512 devices in a mesh: line: 8 (over x, core), surf: 64 (over z, y).
Axes of the slice: x: 4, y: 4, z: 16, core: 2. Of those that a mesh axis runs over, the one named last changes fastest.
Arguments:
- residual: float32 [64, 13, 16384], P('line', None, 'surf'), may hold values from -0.6 to 0.6
- previous: float32 [64, 13, 16384], P('line', None, 'surf'), may hold values from -6 to 6
- edge_blocks: bfloat16 [64, 13, 13, 16384], P('line', None, None, 'surf'), as said below
- damping: float32 [64, 13, 16384], P('line', None, 'surf'), may hold values from 0.004 to 0.016
- lateral: float32 [64, 4, 16384], P('line', None, 'surf'), may hold values from 0.004 to 0.04
- coupling: float32 [13, 13], replicated, may hold values from -1.75 to 1.75
- wall_flags: int32 [16384], P('surf'), may hold values 0 or 1
- wall_gain: float32 [13], replicated, may hold values from 0.5 to 4
- face_table: int32 [64, 4, 2], P('surf'), may hold values from 0 to 63, as said below
Outputs:
- updated: float32 [64, 13, 16384], P('line', None, 'surf')
The draws below stay inside these ranges and needn't reach their ends.
Inputs may be any that keep to these rules, and one draw needn't show every extreme that they name: Each edge_blocks[i, :, :, s] is symmetric, and each of its diagonal entries exceeds the sum of magnitudes of the other entries of its row by more than 0.25. `face_table`: entry [p, f] is (q, r): face f of patch p meets face f xor 1 of patch q, positions mirrored if r is 1; the relation is symmetric with the same r on both sides; the four peers of a patch are four different patches, none the patch itself.
All inputs are finite; a program needn't handle non-finite values. No bound on the sum of `wall_flags` on one device may be relied on, other than what follows from the above.
Results may differ from the reference program's by a relative error of at most 0.0003.
Values sent between devices are 32-bit elements; how exact they have to be, the bound alone decides.
A program may use at most 128 MiB of HBM per device.

```python
import math
import jax
import jax.numpy as jnp
from jax import lax

NSPEC = 13
PW = 16
NPATCH = 64
LINES = 16384
NL = 64


def draw_edge_blocks(key, part):
    key = jax.random.fold_in(key, 11)
    key_off, key_diag = jax.random.split(key)
    raw_entries = jax.random.uniform(key_off, (NL, NSPEC, NSPEC, LINES), jnp.float32, -0.1, 0.1)
    symmetric = 0.5 * (raw_entries + jnp.swapaxes(raw_entries, 1, 2))
    diagonal = 1.2 + jax.random.uniform(key_diag, (NL, NSPEC, LINES), jnp.float32, 0.3, 1.5)
    identity = jnp.eye(NSPEC, dtype=jnp.float32)[None, :, :, None]
    blocks = symmetric * (1.0 - identity) + identity * diagonal[:, :, None, :]
    return blocks.astype(jnp.bfloat16)


def draw_face_table(key, part):
    key = jax.random.fold_in(key, 5)
    key_order, key_rows, key_cols = jax.random.split(key, 3)
    order = jax.random.permutation(key_order, NPATCH).astype(jnp.int32)
    across = NPATCH // 4
    position = jnp.arange(NPATCH, dtype=jnp.int32)
    upper_pos = (position // across + 1) % 4 * across + position % across
    side_pos = position // across * across + (position % across + 1) % across
    row_flip = jax.random.randint(key_rows, (NPATCH,), 0, 2).astype(jnp.int32)
    col_flip = jax.random.randint(key_cols, (NPATCH,), 0, 2).astype(jnp.int32)
    table = jnp.zeros((NPATCH, 4, 2), jnp.int32)
    table = table.at[order, 1, 0].set(order[upper_pos])
    table = table.at[order, 1, 1].set(row_flip)
    table = table.at[order[upper_pos], 0, 0].set(order)
    table = table.at[order[upper_pos], 0, 1].set(row_flip)
    table = table.at[order, 3, 0].set(order[side_pos])
    table = table.at[order, 3, 1].set(col_flip)
    table = table.at[order[side_pos], 2, 0].set(order)
    table = table.at[order[side_pos], 2, 1].set(col_flip)
    return table.astype(jnp.int32)


def touch_ends(array, stream_key, smallest, top_value):
    longest = array.shape.index(max(array.shape))
    spots = []
    for shift in (0, 1):
        where = [jax.random.randint(jax.random.fold_in(stream_key, axis), (), 0, length) for axis, length in enumerate(array.shape)]
        where[longest] = (where[longest] + shift) % array.shape[longest]
        spots.append(tuple(where))
    return array.at[spots[0]].set(smallest).at[spots[1]].set(top_value)


def level_of(own_key, shape, shards, least, largest):
    loudness = 1.0
    for dim, parts in shards:
        steps = jax.random.uniform(jax.random.fold_in(jax.random.fold_in(own_key, 6), dim), (parts,), jnp.float32, least / len(shards), largest / len(shards))
        loudness = loudness * jnp.repeat(jnp.exp(steps), shape[dim] // parts).reshape((-1,) + (1,) * (len(shape) - 1 - dim))
    return loudness


def centred(rng, dims, spread, bound, shards=(), held_as=jnp.bfloat16):
    values = jax.random.normal(rng, dims, jnp.float32) * spread
    if len(shards) > 0:
        values = level_of(rng, dims, shards, -0.22, 0.18) * values
    return jnp.clip(values, min=-bound, max=bound).astype(held_as)


def setup_inputs(seed: int = 0) -> dict:
    streams_of = jax.random.split(jax.random.key(seed), 10)
    residual = centred(streams_of[0], (NL, NSPEC, LINES), 0.1, 0.6, ((0, 8), (2, 64)), jnp.float32)
    previous = centred(streams_of[1], (NL, NSPEC, LINES), 1.0, 6.0, ((0, 8), (2, 64)), jnp.float32)
    edge_blocks = draw_edge_blocks(jax.random.fold_in(streams_of[9], 71), 0)
    damping = jnp.clip(jnp.exp(math.log(0.016) - 1.3862944 * jax.random.uniform(streams_of[3], (NL, NSPEC, LINES), jnp.float32) ** level_of(streams_of[3], (NL, NSPEC, LINES), ((0, 8), (2, 64)), -0.2, 0.2)), 0.004, 0.016)
    lateral = jnp.clip(jnp.exp(math.log(0.04) - 2.30258502 * jax.random.uniform(streams_of[4], (NL, 4, LINES), jnp.float32) ** level_of(streams_of[4], (NL, 4, LINES), ((0, 8), (2, 64)), -0.2, 0.2)), 0.004, 0.04)
    coupling = centred(streams_of[5], (NSPEC, NSPEC), NSPEC ** -0.5, 1.75, (), jnp.float32)
    wall_flags = touch_ends((jax.random.randint(streams_of[6], (LINES,), 0, 2) < 1).astype(jnp.int32), jax.random.fold_in(streams_of[6], 1), 0, 1)
    wall_gain = jnp.clip(jnp.exp(jax.random.uniform(streams_of[7], (NSPEC,), jnp.float32, math.log(0.5), math.log(4.0))), 0.5, 4.0)
    face_table = draw_face_table(jax.random.fold_in(streams_of[9], 71), 0)
    return dict(residual=residual, previous=previous, edge_blocks=edge_blocks, damping=damping, lateral=lateral, coupling=coupling, wall_flags=wall_flags, wall_gain=wall_gain, face_table=face_table)


PRECISE = lax.Precision.HIGHEST

def neighbours(face_table):
    per_patch = PW * PW
    line_index = jnp.arange(NPATCH * per_patch, dtype=jnp.int32)
    patch_id = line_index // per_patch
    within = line_index % per_patch
    row_at = within // PW
    column = within % PW
    peer_patch = face_table[:, :, 0]
    reversed_face = face_table[:, :, 1]
    along_row = jnp.where(reversed_face[patch_id, 0] == 1, PW - 1 - column, column)
    lower_row = jnp.where(row_at > 0, line_index - PW, peer_patch[patch_id, 0] * per_patch + (PW - 1) * PW + along_row)
    along_row = jnp.where(reversed_face[patch_id, 1] == 1, PW - 1 - column, column)
    upper_row = jnp.where(row_at < PW - 1, line_index + PW, peer_patch[patch_id, 1] * per_patch + along_row)
    along_col = jnp.where(reversed_face[patch_id, 2] == 1, PW - 1 - row_at, row_at)
    lower_col = jnp.where(column > 0, line_index - 1, peer_patch[patch_id, 2] * per_patch + along_col * PW + PW - 1)
    along_col = jnp.where(reversed_face[patch_id, 3] == 1, PW - 1 - row_at, row_at)
    upper_col = jnp.where(column < PW - 1, line_index + 1, peer_patch[patch_id, 3] * per_patch + along_col * PW)
    return (lower_row, upper_row, lower_col, upper_col)

def lateral_term(update, beside, lateral, coupling):
    weighted = jnp.zeros_like(update)
    for direction in range(4):
        weighted = weighted + lateral[:, direction, None, :] * jnp.take(update, beside[direction], axis=2)
    return jnp.einsum('ab,ibs->ias', coupling, weighted, precision=PRECISE)

def line_solve(edge_blocks, damping, wall_diag, source_all):
    cell_count = source_all.shape[0]
    line_count = source_all.shape[2]
    identity = jnp.eye(NSPEC, dtype=jnp.float32)

    def edge_at(cell):
        block_here = lax.dynamic_index_in_dim(edge_blocks, cell, 0, keepdims=False).astype(jnp.float32)
        return jnp.transpose(block_here, (2, 0, 1))

    def forward(carry, cell):
        factor_prev, partial_prev = carry
        block_here = edge_at(cell)
        block_above = edge_at(jnp.minimum(cell + 1, cell_count - 1)) * (cell < cell_count - 1).astype(jnp.float32)
        diagonal = lax.dynamic_index_in_dim(damping, cell, 0, keepdims=False) + wall_diag * (cell == 0).astype(jnp.float32)
        block_below = block_here * (cell > 0).astype(jnp.float32)
        pivot_block = block_here + block_above + identity[None] * jnp.transpose(diagonal)[:, None, :]
        pivot_block = pivot_block - jnp.matmul(block_below, factor_prev, precision=PRECISE)
        source = jnp.transpose(lax.dynamic_index_in_dim(source_all, cell, 0, keepdims=False))
        source = source + jnp.matmul(block_below, partial_prev[:, :, None], precision=PRECISE)[:, :, 0]
        partial_value = jnp.linalg.solve(pivot_block, source[:, :, None])[:, :, 0]
        factor = jnp.linalg.solve(pivot_block, block_above)
        return ((factor, partial_value), (factor, partial_value))
    initial = (jnp.zeros((line_count, NSPEC, NSPEC), jnp.float32), jnp.zeros((line_count, NSPEC), jnp.float32))
    _, (factors, partials) = lax.scan(forward, initial, jnp.arange(cell_count, dtype=jnp.int32))

    def backward(solved_next, stored):
        factor, partial_value = stored
        solved_here = partial_value + jnp.matmul(factor, solved_next[:, :, None], precision=PRECISE)[:, :, 0]
        return (solved_here, solved_here)
    _, solved = lax.scan(backward, jnp.zeros((line_count, NSPEC), jnp.float32), (factors, partials), reverse=True)
    return jnp.transpose(solved, (0, 2, 1))

def reference(residual, previous, edge_blocks, damping, lateral, coupling, wall_flags, wall_gain, face_table):
    beside = neighbours(face_table)
    wall_diag = wall_gain[:, None] * wall_flags.astype(jnp.float32)[None, :]
    sweep_one = line_solve(edge_blocks, damping, wall_diag, residual - lateral_term(previous, beside, lateral, coupling))
    return line_solve(edge_blocks, damping, wall_diag, residual - lateral_term(sweep_one, beside, lateral, coupling))
```

```python
import functools

import jax
import jax.numpy as jnp
from jax import lax
from jax.experimental import pallas as pl
from jax.experimental.pallas import tpu as pltpu
from jax.sharding import PartitionSpec as P

N = 13
PW = 16
NY = 4
NZ = 16
NLINE = 8
FB = 56
MROWS = 176
VROWS = 16
MESH = pl.DeviceIdType.MESH
F32 = jnp.float32
BF16 = jnp.bfloat16


def sub_of(shape):
    return lax.broadcasted_iota(jnp.int32, shape, len(shape) - 2)


def lane_of(shape):
    return lax.broadcasted_iota(jnp.int32, shape, len(shape) - 1)


def sroll(x, k):
    return pltpu.roll(x, k % 8, x.ndim - 2)


def lroll(x, k):
    return pltpu.roll(x, k % x.shape[-1], x.ndim - 1)


def mm(out, a, b, ta=False):
    def rows(at):
        acc = [None] * len(at)
        for k in range(N):
            bk = b[k]
            for n, i in enumerate(at):
                term = (a[k, i] if ta else a[i, k])[None] * bk
                acc[n] = term if k == 0 else acc[n] + term
        for n, i in enumerate(at):
            out[i] = acc[n]

    def pair(q, carry):
        rows([2 * q, 2 * q + 1])
        return carry

    lax.fori_loop(0, N // 2, pair, 0)
    rows([N - 1])


def inverse(src, dst):
    a = [src[i, pl.ds(i, N - i)] for i in range(N)]
    for p in range(N):
        d = 1.0 / a[p][0:1]
        parts = [a[i][p - i : p - i + 1] for i in range(p)] + [a[p]]
        col = jnp.concatenate(parts, axis=0) if p else a[p]
        scaled = col * d
        for i in range(N):
            if i == p:
                continue
            new = a[i] - col[i : i + 1] * scaled[i:]
            if i < p:
                pieces = [new[: p - i], scaled[i : i + 1]]
                if p - i + 1 < N - i:
                    pieces.append(new[p - i + 1 :])
                new = jnp.concatenate(pieces, axis=0)
            a[i] = new
        a[p] = jnp.concatenate([-d, scaled[p + 1 :]], axis=0) if p + 1 < N else -d
    for i in range(N):
        neg = -a[i]
        dst[i, pl.ds(i, N - i)] = neg
        for j in range(i + 1, N):
            dst[j, i] = neg[j - i]


def mvt(g, x):
    acc = x[0:1] * g[0]
    for k in range(1, N):
        acc = acc + x[k : k + 1] * g[k]
    return acc


def mv(g, x):
    acc = x[0:1] * g[:, 0]
    for k in range(1, N):
        acc = acc + x[k : k + 1] * g[:, k]
    return acc


def exchange_groups(v):
    which = (lane_of((8, 128)) // 32 - sub_of((8, 128)) // 2 + 4) % 4
    out = v
    for step in range(1, 4):
        out = jnp.where((which == step)[None], sroll(lroll(v, 32 * step), -2 * step), out)
    return out


def split_cells(v):
    h0, h1 = v[:, :, :128], v[:, :, 128:]
    even = (sub_of((8, 128)) % 2 == 0)[None]
    return jnp.where(even, h0, sroll(h1, 1)), jnp.where(even, sroll(h0, -1), h1)


def join_cells(xe, xo):
    even = (sub_of((8, 128)) % 2 == 0)[None]
    h0 = jnp.where(even, xe, sroll(xo, 1))
    h1 = jnp.where(even, sroll(xe, -1), xo)
    return jnp.concatenate([h0, h1], axis=2)


def three_parts(x):
    high = x.astype(BF16).astype(F32)
    rest = x - high
    mid = rest.astype(BF16).astype(F32)
    return jnp.concatenate([high, mid, rest - mid], axis=0).astype(BF16)


def kernel(
    res, prev, edge, damp, lat, coup, flags, gain, tab_v, tab_s, out,
    mats, work, zg0, zg1, yb0, yb1, ysend, tscr, tsm, pick, spread, lsc, wts, inner, field,
    fs, fr, vs, vr, bs, br,
    zss, zrs, yss, yrs, tss, trs, fss, frs, vss, vrs, bss, brs, lsem,
):
    zgs, ybs = (zg0, zg1), (yb0, yb1)
    place = lax.axis_index("line")
    patch = lax.axis_index("surf")
    z, y = patch // NY, patch % NY

    def line_dev(k):
        return (lax.rem(place + k, NLINE), patch)

    def z_dev(k):
        return (place, lax.rem(z + k + NZ, NZ) * NY + y)

    def y_dev(k):
        return (place, z * NY + lax.rem(y + k, NY))

    barrier = pltpu.get_barrier_semaphore()
    friends = [line_dev(k) for k in range(1, NLINE)]
    friends += [z_dev(k) for k in (1, 2, 3, -1, -2, -3)]
    friends += [y_dev(k) for k in range(1, NY)]
    for friend in friends:
        pl.semaphore_signal(barrier, inc=1, device_id=friend, device_id_type=MESH)

    sent = []

    def send(src, dst, ssem, rsem, target):
        copy = pltpu.make_async_remote_copy(
            src_ref=src, dst_ref=dst, send_sem=ssem, recv_sem=rsem, device_id=target, device_id_type=MESH
        )
        copy.start()
        sent.append(copy)
        return copy

    tile = (8, 128)
    sub, lane = sub_of(tile), lane_of(tile)
    slot = sub // 2

    line = lax.broadcasted_iota(jnp.int32, (512, 128), 0)
    col = lax.broadcasted_iota(jnp.int32, (512, 128), 1)
    face, pos = (col // 16) % 4, col % 16
    row_at, col_at = (line % 256) // PW, line % PW
    across = jnp.where(face < 2, row_at, col_at)
    along = jnp.where(face < 2, col_at, row_at)
    hit = (across == (face % 2) * (PW - 1)) & (along == pos) & (line // 256 == col // 64)
    pick[...] = jnp.where(hit, 1.0, 0.0).astype(BF16)

    def borders(values):
        low = values[0:7].reshape(FB, 256)
        high = jnp.concatenate([values[7:N], jnp.zeros((1, 8, 256), F32)], axis=0).reshape(FB, 256)
        wide = jnp.concatenate([low, high], axis=1)
        got = jnp.dot(three_parts(wide), pick[...], preferred_element_type=F32)
        return got[0:FB] + got[FB : 2 * FB] + got[2 * FB :]

    def z_send(ph, d, dist, hop):
        at = lax.rem(z - d * (dist - hop) + NZ, NZ)
        side = 0 if d > 0 else 1
        return send(
            zgs[ph].at[at], zgs[ph].at[at], zss.at[ph, side, dist - 1], zrs.at[ph, side, dist - 1], z_dev(d * hop)
        )

    def z_step(ph, number, flying):
        if number == 0:
            plan = [(d, hop, hop) for hop in (3, 2, 1) for d in (1, -1)]
        elif number == 1:
            for d in (1, -1):
                flying.pop((d, 3)).wait_recv()
            plan = [(d, 3 + hop, hop) for hop in (3, 2, 1) for d in (1, -1)]
        else:
            for d in (1, -1):
                flying.pop((d, 6)).wait_recv()
            plan = [(1, 8, 2), (1, 7, 1), (-1, 7, 1)]
        for d, dist, hop in plan:
            flying[(d, dist)] = z_send(ph, d, dist, hop)

    group = (lane_of((FB, 128)) // 16) % 4

    def choose(blocks):
        got = jnp.where(group == 1, blocks[0], jnp.where(group == 0, blocks[1], jnp.where(group == 3, blocks[2], blocks[3])))
        return got

    def y_phase(ph, flying):
        for copy in flying.values():
            copy.wait_recv()
        arriving = []
        for k in (2, 1, 3, 0):
            to = lax.rem(y + k, NY)
            block = choose([zgs[ph][tsm[to, 0, f] // NY] for f in range(4)])
            if k == 0:
                ybs[ph][y] = block
            else:
                ysend[ph, k - 1] = block
                arriving.append(
                    send(ysend.at[ph, k - 1], ybs[ph].at[y], yss.at[ph, k - 1], yrs.at[ph, k - 1], y_dev(k))
                )
        return arriving

    def ghosts(ph, arriving):
        for copy in arriving:
            copy.wait_recv()
        block = choose([ybs[ph][tsm[y, 0, f] % NY] for f in range(4)])
        got = jnp.dot(three_parts(block), spread[...], preferred_element_type=F32)
        got = got[0:FB] + got[FB : 2 * FB] + got[2 * FB :]
        return got

    def all_to_all(src, dst, rows, ssem, rsem):
        own = pl.multiple_of(place * rows, 8)
        arriving = []
        for k in (4, 3, 5, 2, 6, 1, 7):
            to = pl.multiple_of(lax.rem(place + k, NLINE) * rows, 8)
            arriving.append(
                send(src.at[pl.ds(to, rows)], dst.at[pl.ds(own, rows)], ssem.at[k - 1], rsem.at[k - 1], line_dev(k))
            )
        dst[pl.ds(own, rows)] = src[pl.ds(own, rows)]
        return arriving

    zg0[z] = borders(prev[...])
    tscr[y] = jnp.zeros(tile, jnp.int32)
    tscr[y, 0:2, 0:4] = tab_v[...]
    pl.semaphore_wait(barrier, len(friends))
    flying = {}
    z_step(0, 0, flying)
    tables = [send(tscr.at[y], tscr.at[y], tss.at[k - 1], trs.at[k - 1], y_dev(k)) for k in range(1, NY)]

    (uo, ue, pm, dd, v1, gl, gr, c1, sl, sr, x2, v2, g2, s2, c2, x3, v3, g3, s3, c3, rc, rd,
     w1, h1, x1r, w2, h2, w3, h3, w4) = [mats.at[n] for n in range(30)]

    def each_row(body):
        def step(i, carry):
            body(i)
            return carry

        lax.fori_loop(0, N, step, 0)

    first = ((sub < 2) & (place == 0))[None]
    even_sub = (sub % 2 == 0)[None]

    def build(i):
        e = edge[i].astype(F32)
        h0, h1 = e[:, :, :128], e[:, :, 128:]
        u = jnp.where(even_sub, h0, sroll(h1, 1))
        o = jnp.where(even_sub, sroll(h0, -1), h1)
        uo[i] = o
        ue[i] = jnp.where(first, 0.0, u)
        pm[i] = u + o
        dd[i] = o + jnp.where((sub < 6)[None], sroll(u, -2), 0.0)

    each_row(build)
    de, do = split_cells(damp[...])
    flag = flags[...].astype(F32)
    wall = jnp.where(sub == 0, flag[:, :128], flag[:, 128:])
    wall = jnp.where(first[0], wall, 0.0)
    for i in range(N):
        pm[i, i] = pm[i, i] + de[i] + wall * gain[i]
        dd[i, i] = dd[i, i] + do[i]
    inverse(pm, v1)
    z_step(0, 1, flying)
    mm(gl, v1, ue)
    mm(gr, v1, uo)
    mm(sl, ue, gl)
    mm(sr, uo, gr)
    mm(c1, ue, gr)
    z_step(0, 2, flying)

    def level(p, x, v, g, s, c, shift):
        inverse(p, v)
        mm(g, v, x)
        mm(s, x, g, True)
        if c is not None:

            def turn(i):
                work[i] = sroll(g[i], -shift)

            each_row(turn)
            mm(c, x, work, True)

    def build(i):
        d = dd[i] - sr[i] - jnp.where((sub < 6)[None], sroll(sl[i], -2), 0.0)
        dd[i] = d
        even = (slot % 2 == 0)[None]
        pm[i] = jnp.where(even, d, sroll(d, 2))
        x2[i] = jnp.where(even, c1[:, i], c1[i])

    each_row(build)
    level(pm, x2, v2, g2, s2, c2, 2)

    for copy in tables:
        copy.wait_recv()
    to_smem = pltpu.make_async_copy(tscr, tsm, lsem)
    to_smem.start()
    to_smem.wait()
    arriving = y_phase(0, flying)

    def build(i):
        d = dd[i] - s2[i] - jnp.where((slot == 1)[None], sroll(s2[i], -2), 0.0)
        dd[i] = d
        low = (slot == 0)[None]
        pm[i] = jnp.where(low, sroll(d, -2), sroll(d, 2))
        x3[i] = jnp.where(low, c2[:, i], c2[i])

    each_row(build)
    level(pm, x3, v3, g3, s3, c3, 4)

    def build(i):
        own = dd[i] - sroll(s3[i], 2)
        push = ue[i] - sl[i] - s2[i] - s3[i]
        v = jnp.where((slot == 0)[None], c3[i], jnp.where((slot == 1)[None], sroll(push, 2), own))
        v = exchange_groups(jnp.where((slot == 2)[None], 0.0, v))
        for j in range(N):
            fs[pl.ds(i * N + j, 8, stride=MROWS), :] = v[j]

    each_row(build)
    blocks = all_to_all(fs, fr, MROWS, fss, frs)

    src = lax.broadcasted_iota(jnp.int32, (128, 1024), 0)
    dst = lax.broadcasted_iota(jnp.int32, (128, 1024), 1)
    face = ((src // 16) % 4) ^ 1
    turned = jnp.where(face == 0, tab_s[1, 0], jnp.where(face == 1, tab_s[1, 1], jnp.where(face == 2, tab_s[1, 2], tab_s[1, 3])))
    line = dst % 256
    across = jnp.where(face < 2, line // PW, line % PW)
    along = jnp.where(face < 2, line % PW, line // PW)
    along = along + turned * (PW - 1 - 2 * along)
    hit = (across == (face % 2) * (PW - 1)) & (along == src % 16)
    hit = hit & (dst // 512 == src // 64) & ((dst // 256) % 2 == face // 2)
    spread[...] = jnp.where(hit, 1.0, 0.0).astype(BF16)

    for c in range(8):
        for h in range(2):
            lsc[h, pl.ds(4 * c, 4), :] = lat[c, :, pl.ds(128 * h, 128)]
    lats = [
        jnp.concatenate([lsc[h, pl.ds(d, 8, stride=4), :] for h in range(2)], axis=1) for d in range(4)
    ]
    line = lane_of((8, 256))
    edges = [line < PW, line >= 256 - PW, line % PW == 0, line % PW == PW - 1]
    for d in range(4):
        wts[d] = jnp.where(edges[d], 0.0, lats[d])
    for kind in range(2):
        wts[4 + kind] = jnp.where(
            edges[2 * kind], lats[2 * kind], jnp.where(edges[2 * kind + 1], lats[2 * kind + 1], 0.0)
        )

    def inside(v):
        for i in range(N):
            x = v[i]
            inner[i] = (
                wts[0] * lroll(x, PW) + wts[1] * lroll(x, -PW) + wts[2] * lroll(x, 1) + wts[3] * lroll(x, -1)
            )

    def right_side(got):
        weighted = []
        for i in range(N):
            at, base = (8 * i, 0) if i < 7 else (8 * (i - 7), 512)
            weighted.append(
                inner[i] + wts[4] * got[at : at + 8, base : base + 256] + wts[5] * got[at : at + 8, base + 256 : base + 512]
            )
        rows = []
        for a in range(N):
            acc = res[a]
            for b in range(N):
                acc = acc - coup[a, b] * weighted[b]
            rows.append(acc[None])
        return jnp.concatenate(rows, axis=0)

    def forward(ph, rhs):
        re, ro = split_cells(rhs)
        ul, ur = mvt(gl, re), mvt(gr, re)
        ro = ro + ur + jnp.where((sub < 6)[None], sroll(ul, -2), 0.0)
        rk2 = jnp.where((slot % 2 == 0)[None], ro, sroll(ro, 2))
        u2 = mvt(g2, rk2)
        ro = ro + u2 + jnp.where((slot == 1)[None], sroll(u2, -2), 0.0)
        rk3 = jnp.where((slot == 0)[None], sroll(ro, -2), sroll(ro, 2))
        u3 = mvt(g3, rk3)
        own = ro + sroll(u3, 2)
        tip = ul + u2 + u3
        v = jnp.where((slot == 1)[None], sroll(tip, 2), jnp.where((slot == 3)[None], own, 0.0))
        v = exchange_groups(v)
        for j in range(N):
            vs[ph, pl.ds(j, 8, stride=VROWS), :] = v[j]
        for j in range(N, VROWS):
            vs[ph, pl.ds(j, 8, stride=VROWS), :] = jnp.zeros(tile, F32)
        arriving = all_to_all(vs.at[ph], vr.at[ph], VROWS, vss.at[ph], vrs.at[ph])
        return re, rk2, rk3, arriving

    def separators(ph, arriving):
        for copy in arriving:
            copy.wait_recv()
        got = jnp.concatenate([vr[ph, pl.ds(j, 8, stride=VROWS), :][None] for j in range(N)], axis=0)
        r = lroll(got, 32) + jnp.where((sub < 7)[None], sroll(lroll(got, 96), -1), 0.0)
        even = (sub % 2 == 0)[None]
        fourth = (sub % 4 == 0)[None]
        rk1 = jnp.where(even, r, sroll(r, 1))
        u = mvt(h1, rk1)
        r = r + u + sroll(u, -1)
        rk2 = jnp.where(fourth, sroll(r, -1), sroll(r, 1))
        u = mvt(h2, rk2)
        r = r + sroll(u, 1) + sroll(u, -1)
        rk3 = sroll(r, 1)
        u = mvt(h3, rk3)
        x7 = mvt(w4, r + sroll(u, 3))
        x3 = sroll(mvt(w3, rk3) + mv(h3, sroll(x7, -3)), -1)
        known = jnp.where((sub == 3)[None], x3, x7)
        near = jnp.where((sub == 2)[None], sroll(x3, -1), jnp.where((sub == 4)[None], sroll(x3, 1), sroll(x7, -1)))
        near = jnp.where((sub == 0)[None], 0.0, near)
        u = mv(h2, near) + jnp.where(fourth, mvt(w2, rk2), 0.0)
        x = jnp.where((sub % 4 == 1)[None], sroll(u, 1) + sroll(u, -1), known)
        near = jnp.where((sub == 0)[None], 0.0, jnp.where(even, sroll(x, 1), x))
        u = mv(h1, near) + jnp.where(even, mvt(w1, rk1), 0.0)
        x = jnp.where(even, u + sroll(u, -1), x)
        below = jnp.where((sub == 0)[None], 0.0, sroll(x, 1))
        quarter = (lane // 32)[None]
        msg = jnp.where(
            quarter == 0, below, jnp.where(quarter == 2, lroll(x, 64), jnp.where(quarter == 3, lroll(x, 96), 0.0))
        )
        for j in range(N):
            bs[ph, pl.ds(j, 8, stride=VROWS), :] = msg[j]
        for j in range(N, VROWS):
            bs[ph, pl.ds(j, 8, stride=VROWS), :] = jnp.zeros(tile, F32)
        return all_to_all(bs.at[ph], br.at[ph], VROWS, bss.at[ph], brs.at[ph])

    def backward(ph, kept, arriving):
        re, rk2, rk3, _ = kept
        y1, y2, y3 = mvt(v1, re), mvt(v2, rk2), mvt(v3, rk3)
        for copy in arriving:
            copy.wait_recv()
        got = jnp.concatenate([br[ph, pl.ds(j, 8, stride=VROWS), :][None] for j in range(N)], axis=0)
        ends = exchange_groups(got)
        u = mv(g3, ends) + jnp.where((slot == 0)[None], y3, 0.0)
        x3 = sroll(u, 2) + sroll(u, -2)
        near = jnp.where((slot == 1)[None], x3, jnp.where((slot == 2)[None], sroll(x3, 2), ends))
        u = mv(g2, near) + jnp.where((slot % 2 == 0)[None], y2, 0.0)
        both = u + sroll(u, -2)
        xo = jnp.where((slot % 2 == 0)[None], both, jnp.where((slot == 1)[None], x3, ends))
        xl = jnp.where((slot == 0)[None], ends, sroll(xo, 2))
        xe = y1 + mv(gl, xl) + mv(gr, xo)
        return join_cells(xe, xo)

    inside(prev)
    rhs = right_side(ghosts(0, arriving))
    kept = forward(0, rhs)

    for copy in blocks:
        copy.wait_recv()

    def build(i):
        rows = []
        for j in range(N):
            rows.append(fr[pl.ds(i * N + j, 8, stride=MROWS), :][None])
        v = jnp.concatenate(rows, axis=0)
        rc[i] = v
        rd[i] = lroll(v, 32) + jnp.where((sub < 7)[None], sroll(lroll(v, 96), -1), 0.0)

    each_row(build)

    def build(i):
        even = (sub % 2 == 0)[None]
        x1r[i] = jnp.where(even, rc[:, i], rc[i])
        pm[i] = jnp.where(even, rd[i], sroll(rd[i], 1))

    each_row(build)
    level(pm, x1r, w1, h1, s3, c3, 1)

    def build(i):
        d = rd[i] - s3[i] - sroll(s3[i], -1)
        rd[i] = d
        fourth = (sub % 4 == 0)[None]
        pm[i] = jnp.where(fourth, sroll(d, -1), sroll(d, 1))
        x2[i] = jnp.where(fourth, c3[:, i], c3[i])

    each_row(build)
    level(pm, x2, w2, h2, s3, c2, 2)

    def build(i):
        d = rd[i] - sroll(s3[i], 1) - sroll(s3[i], -1)
        rd[i] = d
        pm[i] = sroll(d, 1)

    each_row(build)
    level(pm, c2, w3, h3, s3, None, 0)

    def build(i):
        pm[i] = rd[i] - sroll(s3[i], 3)

    each_row(build)
    inverse(pm, w4)

    back = separators(0, kept[3])
    first_sweep = backward(0, kept, back)
    zg1[z] = borders(first_sweep)
    field[...] = first_sweep
    flying = {}
    z_step(1, 0, flying)
    inside(field)
    z_step(1, 1, flying)
    z_step(1, 2, flying)
    arriving = y_phase(1, flying)
    rhs = right_side(ghosts(1, arriving))
    kept = forward(1, rhs)
    back = separators(1, kept[3])
    out[...] = backward(1, kept, back)

    for copy in sent:
        copy.wait_send()


def body(residual, previous, edge_blocks, damping, lateral, coupling, wall_flags, wall_gain, face_table):
    def by_unknown(v):
        return jnp.transpose(v, (1, 0, 2))

    table = jnp.transpose(face_table[0])
    vmem = pl.BlockSpec(memory_space=pltpu.VMEM)
    smem = pl.BlockSpec(memory_space=pltpu.SMEM)
    dma = pltpu.SemaphoreType.DMA
    got = pl.pallas_call(
        kernel,
        out_shape=jax.ShapeDtypeStruct((N, 8, 256), F32),
        in_specs=[vmem, vmem, vmem, vmem, vmem, smem, vmem, smem, vmem, smem],
        out_specs=vmem,
        scratch_shapes=[
            pltpu.VMEM((30, N, N, 8, 128), F32),
            pltpu.VMEM((N, N, 8, 128), F32),
            pltpu.VMEM((NZ, FB, 128), F32),
            pltpu.VMEM((NZ, FB, 128), F32),
            pltpu.VMEM((NY, FB, 128), F32),
            pltpu.VMEM((NY, FB, 128), F32),
            pltpu.VMEM((2, NY - 1, FB, 128), F32),
            pltpu.VMEM((NY, 8, 128), jnp.int32),
            pltpu.SMEM((NY, 8, 128), jnp.int32),
            pltpu.VMEM((512, 128), BF16),
            pltpu.VMEM((128, 1024), BF16),
            pltpu.VMEM((2, 32, 128), F32),
            pltpu.VMEM((6, 8, 256), F32),
            pltpu.VMEM((N, 8, 256), F32),
            pltpu.VMEM((N, 8, 256), F32),
            pltpu.VMEM((NLINE * MROWS, 128), F32),
            pltpu.VMEM((NLINE * MROWS, 128), F32),
            pltpu.VMEM((2, NLINE * VROWS, 128), F32),
            pltpu.VMEM((2, NLINE * VROWS, 128), F32),
            pltpu.VMEM((2, NLINE * VROWS, 128), F32),
            pltpu.VMEM((2, NLINE * VROWS, 128), F32),
            dma((2, 2, 8)),
            dma((2, 2, 8)),
            dma((2, NY - 1)),
            dma((2, NY - 1)),
            dma((NY - 1,)),
            dma((NY - 1,)),
            dma((NLINE - 1,)),
            dma((NLINE - 1,)),
            dma((2, NLINE - 1)),
            dma((2, NLINE - 1)),
            dma((2, NLINE - 1)),
            dma((2, NLINE - 1)),
            dma,
        ],
        compiler_params=pltpu.CompilerParams(
            collective_id=0, has_side_effects=True, vmem_limit_bytes=48 * 1024 * 1024
        ),
        name="line_sweeps",
    )(
        by_unknown(residual),
        by_unknown(previous),
        jnp.transpose(edge_blocks, (1, 2, 0, 3)),
        by_unknown(damping),
        lateral,
        coupling,
        wall_flags.reshape(1, 256),
        wall_gain,
        table,
        table,
    )
    return jnp.transpose(got, (1, 0, 2))


def solution(mesh):
    placed = (
        P("line", None, "surf"),
        P("line", None, "surf"),
        P("line", None, None, "surf"),
        P("line", None, "surf"),
        P("line", None, "surf"),
        P(),
        P("surf"),
        P(),
        P("surf", None, None),
    )
    return jax.shard_map(
        body, mesh=mesh, in_specs=placed, out_specs=P("line", None, "surf"), check_vma=False
    )
```

```python
import functools

import jax
import jax.numpy as jnp
from jax import lax
from jax.experimental import pallas as pl
from jax.experimental.pallas import tpu as pltpu
from jax.sharding import PartitionSpec as P

N = 13
PW = 16
NY = 4
NZ = 16
NLINE = 8
FB = 56
MROWS = 96
VROWS = 16
MESH = pl.DeviceIdType.MESH
F32 = jnp.float32
BF16 = jnp.bfloat16


def sub_of(shape):
    return lax.broadcasted_iota(jnp.int32, shape, len(shape) - 2)


def lane_of(shape):
    return lax.broadcasted_iota(jnp.int32, shape, len(shape) - 1)


def sroll(x, k):
    return pltpu.roll(x, k % 8, x.ndim - 2)


def lroll(x, k):
    return pltpu.roll(x, k % x.shape[-1], x.ndim - 1)


def mm(out, a, b, ta=False):
    def rows(at):
        acc = [None] * len(at)
        for k in range(N):
            bk = b[k]
            for n, i in enumerate(at):
                term = (a[k, i] if ta else a[i, k])[None] * bk
                acc[n] = term if k == 0 else acc[n] + term
        for n, i in enumerate(at):
            out[i] = acc[n]

    def pair(q, carry):
        rows([2 * q, 2 * q + 1])
        return carry

    lax.fori_loop(0, N // 2, pair, 0)
    rows([N - 1])


def mm_upper(out, a, b):
    for top in range(0, N, 2):
        at = [i for i in (top, top + 1) if i < N]
        acc = [None] * len(at)
        for k in range(N):
            bk = b[k, pl.ds(top, N - top)]
            for n, i in enumerate(at):
                term = a[k, i][None] * bk
                acc[n] = term if k == 0 else acc[n] + term
        for n, i in enumerate(at):
            out[i, pl.ds(top, N - top)] = acc[n]


def mm_split(out, a, b, ta=False, shift=0, upper=False):
    for at in (range(0, 4), range(4, 8), range(8, N)):
        low = at[0] // 4 if upper else 0
        acc = [None] * len(at)
        for k in range(N):
            bk = b[k, pl.ds(low, 4 - low)]
            if shift:
                bk = sroll(bk, -shift)
            for n, i in enumerate(at):
                term = (a[k, i] if ta else a[i, k])[None] * bk
                acc[n] = term if k == 0 else acc[n] + term
        for n, i in enumerate(at):
            out[i, pl.ds(low, 4 - low)] = acc[n]


def spread_groups(v):
    turns = [v] + [lroll(v, 32 * k) for k in range(1, 4)]
    quarter = (lane_of((8, 128)) // 32)[None]
    got = []
    for g in range(4):
        x = turns[3]
        for k in range(3):
            x = jnp.where(quarter == (g + k) % 4, turns[k], x)
        got.append(x)
    return got


def inverse(src, dst):
    a = [src[i, pl.ds(i, N - i)] for i in range(N)]
    for p in range(N):
        d = 1.0 / a[p][0:1]
        parts = [a[i][p - i : p - i + 1] for i in range(p)] + [a[p]]
        col = jnp.concatenate(parts, axis=0) if p else a[p]
        scaled = col * d
        for i in range(N):
            if i == p:
                continue
            new = a[i] - col[i : i + 1] * scaled[i:]
            if i < p:
                pieces = [new[: p - i], scaled[i : i + 1]]
                if p - i + 1 < N - i:
                    pieces.append(new[p - i + 1 :])
                new = jnp.concatenate(pieces, axis=0)
            a[i] = new
        a[p] = jnp.concatenate([-d, scaled[p + 1 :]], axis=0) if p + 1 < N else -d
    for i in range(N):
        neg = -a[i]
        dst[i, pl.ds(i, N - i)] = neg
        for j in range(i + 1, N):
            dst[j, i] = neg[j - i]


def mvt(g, x):
    acc = x[0:1] * g[0]
    for k in range(1, N):
        acc = acc + x[k : k + 1] * g[k]
    return acc


def mv(g, x):
    acc = x[0:1] * g[:, 0]
    for k in range(1, N):
        acc = acc + x[k : k + 1] * g[:, k]
    return acc


def exchange_groups(v):
    which = (lane_of((8, 128)) // 32 - sub_of((8, 128)) // 2 + 4) % 4
    out = v
    for step in range(1, 4):
        out = jnp.where((which == step)[None], sroll(lroll(v, 32 * step), -2 * step), out)
    return out


def split_cells(v):
    h0, h1 = v[:, :, :128], v[:, :, 128:]
    even = (sub_of((8, 128)) % 2 == 0)[None]
    return jnp.where(even, h0, sroll(h1, 1)), jnp.where(even, sroll(h0, -1), h1)


def join_cells(xe, xo):
    even = (sub_of((8, 128)) % 2 == 0)[None]
    h0 = jnp.where(even, xe, sroll(xo, 1))
    h1 = jnp.where(even, sroll(xe, -1), xo)
    return jnp.concatenate([h0, h1], axis=2)


def three_parts(x):
    high = x.astype(BF16).astype(F32)
    rest = x - high
    mid = rest.astype(BF16).astype(F32)
    return jnp.concatenate([high, mid, rest - mid], axis=0).astype(BF16)


def kernel(
    res_any, prev_any, edge_any, damp_any, lat_any, coup, flags, gain, tab_v, tab_s, out,
    res, prev, edge, damp, lat, ins, mats, work, thin, zg0, zg1, yb0, yb1, ysend, tscr, tsm, pick, spread, lsc, wts, inner, field,
    fs, fr, vs, vr, bs, br,
    zss, zrs, yss, yrs, tss, trs, fss, frs, vss, vrs, bss, brs, lsem,
):
    zgs, ybs = (zg0, zg1), (yb0, yb1)
    loads = {}
    pairs = dict(prev=(prev_any, prev), edge=(edge_any, edge), damp=(damp_any, damp), lat=(lat_any, lat), res=(res_any, res))
    for n, (name, (far, near)) in enumerate(pairs.items()):
        loads[name] = pltpu.make_async_copy(far, near, ins.at[n])
        loads[name].start()
    place = lax.axis_index("line")
    patch = lax.axis_index("surf")
    z, y = patch // NY, patch % NY

    def line_dev(k):
        return (lax.rem(place + k, NLINE), patch)

    def z_dev(k):
        return (place, lax.rem(z + k + NZ, NZ) * NY + y)

    def y_dev(k):
        return (place, z * NY + lax.rem(y + k, NY))

    barrier = pltpu.get_barrier_semaphore()
    friends = [line_dev(k) for k in range(1, NLINE)]
    friends += [z_dev(k) for k in (1, 2, 3, -1, -2, -3)]
    friends += [y_dev(k) for k in range(1, NY)]
    for friend in friends:
        pl.semaphore_signal(barrier, inc=1, device_id=friend, device_id_type=MESH)

    sent = []

    def send(src, dst, ssem, rsem, target):
        copy = pltpu.make_async_remote_copy(
            src_ref=src, dst_ref=dst, send_sem=ssem, recv_sem=rsem, device_id=target, device_id_type=MESH
        )
        copy.start()
        sent.append(copy)
        return copy

    tile = (8, 128)
    sub, lane = sub_of(tile), lane_of(tile)
    slot = sub // 2

    line = lax.broadcasted_iota(jnp.int32, (512, 128), 0)
    col = lax.broadcasted_iota(jnp.int32, (512, 128), 1)
    face, pos = (col // 16) % 4, col % 16
    row_at, col_at = (line % 256) // PW, line % PW
    across = jnp.where(face < 2, row_at, col_at)
    along = jnp.where(face < 2, col_at, row_at)
    hit = (across == (face % 2) * (PW - 1)) & (along == pos) & (line // 256 == col // 64)
    pick[...] = jnp.where(hit, 1.0, 0.0).astype(BF16)

    def borders(values):
        low = values[0:7].reshape(FB, 256)
        high = jnp.concatenate([values[7:N], jnp.zeros((1, 8, 256), F32)], axis=0).reshape(FB, 256)
        wide = jnp.concatenate([low, high], axis=1)
        got = jnp.dot(three_parts(wide), pick[...], preferred_element_type=F32)
        return got[0:FB] + got[FB : 2 * FB] + got[2 * FB :]

    def z_send(ph, d, dist, hop):
        at = lax.rem(z - d * (dist - hop) + NZ, NZ)
        side = 0 if d > 0 else 1
        return send(
            zgs[ph].at[at], zgs[ph].at[at], zss.at[ph, side, dist - 1], zrs.at[ph, side, dist - 1], z_dev(d * hop)
        )

    def z_step(ph, number, flying):
        waited, plan = (
            (0, ((3, 3), (1, 1))),
            (1, ((2, 1),)),
            (3, ((6, 3), (4, 1))),
            (4, ((5, 1),)),
            (6, ((8, 2), (7, 1))),
        )[number]
        if waited:
            for d in (1, -1):
                flying.pop((d, waited)).wait_recv()
        for dist, hop in plan:
            for d in (1, -1):
                if d > 0 or dist < 8:
                    flying[(d, dist)] = z_send(ph, d, dist, hop)

    group = (lane_of((FB, 128)) // 16) % 4

    def choose(blocks):
        got = jnp.where(group == 1, blocks[0], jnp.where(group == 0, blocks[1], jnp.where(group == 3, blocks[2], blocks[3])))
        return got

    def y_phase(ph, flying):
        for copy in flying.values():
            copy.wait_recv()
        arriving = []
        for k in (2, 1, 3, 0):
            to = lax.rem(y + k, NY)
            block = choose([zgs[ph][tsm[to, 0, f] // NY] for f in range(4)])
            if k == 0:
                ybs[ph][y] = block
            else:
                ysend[ph, k - 1] = block
                arriving.append(
                    send(ysend.at[ph, k - 1], ybs[ph].at[y], yss.at[ph, k - 1], yrs.at[ph, k - 1], y_dev(k))
                )
        return arriving

    def ghosts(ph, arriving):
        for copy in arriving:
            copy.wait_recv()
        block = choose([ybs[ph][tsm[y, 0, f] % NY] for f in range(4)])
        got = jnp.dot(three_parts(block), spread[...], preferred_element_type=F32)
        got = got[0:FB] + got[FB : 2 * FB] + got[2 * FB :]
        return got

    def all_to_all(src, dst, rows, ssem, rsem):
        own = pl.multiple_of(place * rows, 8)
        arriving = []
        for k in (4, 3, 5, 2, 6, 1, 7):
            to = pl.multiple_of(lax.rem(place + k, NLINE) * rows, 8)
            arriving.append(
                send(src.at[pl.ds(to, rows)], dst.at[pl.ds(own, rows)], ssem.at[k - 1], rsem.at[k - 1], line_dev(k))
            )
        dst[pl.ds(own, rows)] = src[pl.ds(own, rows)]
        return arriving

    loads["prev"].wait()
    zg0[z] = borders(prev[...])
    tscr[y] = jnp.zeros(tile, jnp.int32)
    tscr[y, 0:2, 0:4] = tab_v[...]
    pl.semaphore_wait(barrier, len(friends))
    flying = {}
    z_step(0, 0, flying)
    tables = [send(tscr.at[y], tscr.at[y], tss.at[k - 1], trs.at[k - 1], y_dev(k)) for k in range(1, NY)]

    (uo, ue, pm, dd, v1, gl, gr, c1, sl, sr, x2, v2, g2, s2, c2, x3, v3, g3, s3, c3, rc, rd,
     w1, h1, x1r, w2, h2, w3, h3, w4) = [mats.at[n] for n in range(30)]

    def each_row(body):
        def step(i, carry):
            body(i)
            return carry

        lax.fori_loop(0, N, step, 0, unroll=True)

    first = ((sub < 2) & (place == 0))[None]
    even_sub = (sub % 2 == 0)[None]

    def build(i):
        e = edge[i].astype(F32)
        h0, h1 = e[:, :, :128], e[:, :, 128:]
        u = jnp.where(even_sub, h0, sroll(h1, 1))
        o = jnp.where(even_sub, sroll(h0, -1), h1)
        uo[i] = o
        ue[i] = jnp.where(first, 0.0, u)
        pm[i] = u + o
        dd[i] = o + jnp.where((sub < 6)[None], sroll(u, -2), 0.0)

    loads["edge"].wait()
    each_row(build)
    loads["damp"].wait()
    de, do = split_cells(damp[...])
    flag = flags[...].astype(F32)
    wall = jnp.where(sub == 0, flag[:, :128], flag[:, 128:])
    wall = jnp.where(first[0], wall, 0.0)
    for i in range(N):
        pm[i, i] = pm[i, i] + de[i] + wall * gain[i]
        dd[i, i] = dd[i, i] + do[i]
    inverse(pm, v1)
    mm(gl, v1, ue)
    mm(gr, v1, uo)
    z_step(0, 1, flying)
    mm_upper(sl, ue, gl)
    mm_upper(sr, uo, gr)
    z_step(0, 2, flying)
    mm(c1, ue, gr)
    z_step(0, 3, flying)

    def level(p, x, v, g, s, c, shift):
        inverse(p, v)
        mm(g, v, x)
        mm_upper(s, x, g)

        def turn(i):
            work[i] = sroll(g[i], -shift)

        each_row(turn)
        mm(c, x, work, True)

    def level_split(p, x, v, g, s, c, shift):
        inverse(p, v)
        xs, gs, ss, cs = [thin.at[n] for n in range(4)]
        quarter = lane // 32

        def split(k):
            for q in range(4):
                got = x[k, 4 * q]
                for n in range(1, min(4, N - 4 * q)):
                    got = jnp.where(quarter == n, x[k, 4 * q + n], got)
                xs[k, q] = got

        each_row(split)
        mm_split(gs, v, xs)
        mm_split(ss, x, gs, True, upper=True)
        if c is not None:
            mm_split(cs, x, gs, True, shift)

        def join(i):
            for q in range(4):
                wide = min(4, N - 4 * q)
                full = spread_groups(ss[i, q][None])
                far = spread_groups(cs[i, q][None]) if c is not None else None
                for n in range(wide):
                    g[i, 4 * q + n] = lroll(gs[i, q], -32 * n) if n else gs[i, q]
                    s[i, 4 * q + n] = full[n][0]
                    if c is not None:
                        c[i, 4 * q + n] = far[n][0]

        each_row(join)

    def build(i):
        d = dd[i] - sr[i] - jnp.where((sub < 6)[None], sroll(sl[i], -2), 0.0)
        dd[i] = d
        even = (slot % 2 == 0)[None]
        pm[i] = jnp.where(even, d, sroll(d, 2))
        x2[i] = jnp.where(even, c1[:, i], c1[i])

    each_row(build)
    level(pm, x2, v2, g2, s2, c2, 2)

    z_step(0, 4, flying)
    for copy in tables:
        copy.wait_recv()
    to_smem = pltpu.make_async_copy(tscr, tsm, lsem)
    to_smem.start()

    def build(i):
        d = dd[i] - s2[i] - jnp.where((slot == 1)[None], sroll(s2[i], -2), 0.0)
        dd[i] = d
        low = (slot == 0)[None]
        pm[i] = jnp.where(low, sroll(d, -2), sroll(d, 2))
        x3[i] = jnp.where(low, c2[:, i], c2[i])

    each_row(build)
    level(pm, x3, v3, g3, s3, c3, 4)

    def build(i):
        own = dd[i] - sroll(s3[i], 2)
        push = ue[:, i] - sl[:, i] - s2[:, i] - s3[:, i]
        cross = c3[i]
        rows = []
        for q in range(7):
            j = 2 * q
            parts = [cross[j], jnp.where(j >= i, sroll(own[j], 4), sroll(push[j], 2))]
            if j + 1 < N:
                parts += [sroll(cross[j + 1], 4), jnp.where(j + 1 >= i, own[j + 1], sroll(push[j + 1], -2))]
            else:
                parts += [jnp.zeros(tile, F32)] * 2
            v = parts[3]
            for t in range(3):
                v = jnp.where(slot == t, parts[t], v)
            rows.append(v[None])
        v = exchange_groups(jnp.concatenate(rows, axis=0))
        for q in range(7):
            fs[pl.ds(i * 7 + q, 8, stride=MROWS), :] = v[q]

    each_row(build)
    rows = []
    for q in range(4):
        v = jnp.zeros(tile, F32)
        for t in range(min(4, N - 4 * q)):
            i = 4 * q + t
            v = jnp.where(slot == t, sroll(ue[i, i] - sl[i, i] - s2[i, i] - s3[i, i], 2 * t), v)
        rows.append(v[None])
    v = exchange_groups(jnp.concatenate(rows, axis=0))
    for q in range(4):
        fs[pl.ds(91 + q, 8, stride=MROWS), :] = v[q]
    fs[pl.ds(95, 8, stride=MROWS), :] = jnp.zeros(tile, F32)
    blocks = all_to_all(fs, fr, MROWS, fss, frs)

    to_smem.wait()
    arriving = y_phase(0, flying)

    src = lax.broadcasted_iota(jnp.int32, (128, 1024), 0)
    dst = lax.broadcasted_iota(jnp.int32, (128, 1024), 1)
    face = ((src // 16) % 4) ^ 1
    turned = jnp.where(face == 0, tab_s[1, 0], jnp.where(face == 1, tab_s[1, 1], jnp.where(face == 2, tab_s[1, 2], tab_s[1, 3])))
    line = dst % 256
    across = jnp.where(face < 2, line // PW, line % PW)
    along = jnp.where(face < 2, line % PW, line // PW)
    along = along + turned * (PW - 1 - 2 * along)
    hit = (across == (face % 2) * (PW - 1)) & (along == src % 16)
    hit = hit & (dst // 512 == src // 64) & ((dst // 256) % 2 == face // 2)
    spread[...] = jnp.where(hit, 1.0, 0.0).astype(BF16)

    loads["lat"].wait()
    loads["res"].wait()
    for c in range(8):
        for h in range(2):
            lsc[h, pl.ds(4 * c, 4), :] = lat[c, :, pl.ds(128 * h, 128)]
    lats = [
        jnp.concatenate([lsc[h, pl.ds(d, 8, stride=4), :] for h in range(2)], axis=1) for d in range(4)
    ]
    line = lane_of((8, 256))
    edges = [line < PW, line >= 256 - PW, line % PW == 0, line % PW == PW - 1]
    for d in range(4):
        wts[d] = jnp.where(edges[d], 0.0, lats[d])
    for kind in range(2):
        wts[4 + kind] = jnp.where(
            edges[2 * kind], lats[2 * kind], jnp.where(edges[2 * kind + 1], lats[2 * kind + 1], 0.0)
        )

    def inside(v):
        for i in range(N):
            x = v[i]
            inner[i] = (
                wts[0] * lroll(x, PW) + wts[1] * lroll(x, -PW) + wts[2] * lroll(x, 1) + wts[3] * lroll(x, -1)
            )

    def right_side(got):
        weighted = []
        for i in range(N):
            at, base = (8 * i, 0) if i < 7 else (8 * (i - 7), 512)
            weighted.append(
                inner[i] + wts[4] * got[at : at + 8, base : base + 256] + wts[5] * got[at : at + 8, base + 256 : base + 512]
            )
        rows = []
        for a in range(N):
            acc = res[a]
            for b in range(N):
                acc = acc - coup[a, b] * weighted[b]
            rows.append(acc[None])
        return jnp.concatenate(rows, axis=0)

    def forward(ph, rhs):
        re, ro = split_cells(rhs)
        ul, ur = mvt(gl, re), mvt(gr, re)
        ro = ro + ur + jnp.where((sub < 6)[None], sroll(ul, -2), 0.0)
        rk2 = jnp.where((slot % 2 == 0)[None], ro, sroll(ro, 2))
        u2 = mvt(g2, rk2)
        ro = ro + u2 + jnp.where((slot == 1)[None], sroll(u2, -2), 0.0)
        rk3 = jnp.where((slot == 0)[None], sroll(ro, -2), sroll(ro, 2))
        u3 = mvt(g3, rk3)
        own = ro + sroll(u3, 2)
        tip = ul + u2 + u3
        v = jnp.where((slot == 1)[None], sroll(tip, 2), jnp.where((slot == 3)[None], own, 0.0))
        v = exchange_groups(v)
        for j in range(N):
            vs[ph, pl.ds(j, 8, stride=VROWS), :] = v[j]
        for j in range(N, VROWS):
            vs[ph, pl.ds(j, 8, stride=VROWS), :] = jnp.zeros(tile, F32)
        arriving = all_to_all(vs.at[ph], vr.at[ph], VROWS, vss.at[ph], vrs.at[ph])
        return re, rk2, rk3, arriving

    def separators(ph, arriving):
        for copy in arriving:
            copy.wait_recv()
        got = jnp.concatenate([vr[ph, pl.ds(j, 8, stride=VROWS), :][None] for j in range(N)], axis=0)
        r = lroll(got, 32) + jnp.where((sub < 7)[None], sroll(lroll(got, 96), -1), 0.0)
        even = (sub % 2 == 0)[None]
        fourth = (sub % 4 == 0)[None]
        rk1 = jnp.where(even, r, sroll(r, 1))
        u = mvt(h1, rk1)
        r = r + u + sroll(u, -1)
        rk2 = jnp.where(fourth, sroll(r, -1), sroll(r, 1))
        u = mvt(h2, rk2)
        r = r + sroll(u, 1) + sroll(u, -1)
        rk3 = sroll(r, 1)
        u = mvt(h3, rk3)
        x7 = mvt(w4, r + sroll(u, 3))
        x3 = sroll(mvt(w3, rk3) + mv(h3, sroll(x7, -3)), -1)
        known = jnp.where((sub == 3)[None], x3, x7)
        near = jnp.where((sub == 2)[None], sroll(x3, -1), jnp.where((sub == 4)[None], sroll(x3, 1), sroll(x7, -1)))
        near = jnp.where((sub == 0)[None], 0.0, near)
        u = mv(h2, near) + jnp.where(fourth, mvt(w2, rk2), 0.0)
        x = jnp.where((sub % 4 == 1)[None], sroll(u, 1) + sroll(u, -1), known)
        near = jnp.where((sub == 0)[None], 0.0, jnp.where(even, sroll(x, 1), x))
        u = mv(h1, near) + jnp.where(even, mvt(w1, rk1), 0.0)
        x = jnp.where(even, u + sroll(u, -1), x)
        below = jnp.where((sub == 0)[None], 0.0, sroll(x, 1))
        quarter = (lane // 32)[None]
        msg = jnp.where(
            quarter == 0, below, jnp.where(quarter == 2, lroll(x, 64), jnp.where(quarter == 3, lroll(x, 96), 0.0))
        )
        for j in range(N):
            bs[ph, pl.ds(j, 8, stride=VROWS), :] = msg[j]
        for j in range(N, VROWS):
            bs[ph, pl.ds(j, 8, stride=VROWS), :] = jnp.zeros(tile, F32)
        return all_to_all(bs.at[ph], br.at[ph], VROWS, bss.at[ph], brs.at[ph])

    def backward(ph, kept, arriving):
        re, rk2, rk3, _ = kept
        y1, y2, y3 = mvt(v1, re), mvt(v2, rk2), mvt(v3, rk3)
        for copy in arriving:
            copy.wait_recv()
        got = jnp.concatenate([br[ph, pl.ds(j, 8, stride=VROWS), :][None] for j in range(N)], axis=0)
        ends = exchange_groups(got)
        u = mv(g3, ends) + jnp.where((slot == 0)[None], y3, 0.0)
        x3 = sroll(u, 2) + sroll(u, -2)
        near = jnp.where((slot == 1)[None], x3, jnp.where((slot == 2)[None], sroll(x3, 2), ends))
        u = mv(g2, near) + jnp.where((slot % 2 == 0)[None], y2, 0.0)
        both = u + sroll(u, -2)
        xo = jnp.where((slot % 2 == 0)[None], both, jnp.where((slot == 1)[None], x3, ends))
        xl = jnp.where((slot == 0)[None], ends, sroll(xo, 2))
        xe = y1 + mv(gl, xl) + mv(gr, xo)
        return join_cells(xe, xo)

    inside(prev)
    rhs = right_side(ghosts(0, arriving))
    kept = forward(0, rhs)

    rt = sr
    for copy in blocks:
        copy.wait_recv()

    def build(i):
        rows = [fr[pl.ds(i * 7 + q, 8, stride=MROWS), :][None] for q in range(7)]
        got = spread_groups(jnp.concatenate(rows, axis=0))
        for j in range(N):
            rc[i, j] = got[j % 2 * 2][j // 2]
            rt[i, j] = got[j % 2 * 2 + 1][j // 2]

    each_row(build)

    def build(i):
        rd[i] = rt[i] + jnp.where((sub < 7)[None], sroll(rt[:, i], -1), 0.0)

    each_row(build)
    rows = [fr[pl.ds(91 + q, 8, stride=MROWS), :][None] for q in range(4)]
    got = spread_groups(jnp.concatenate(rows, axis=0))
    for i in range(N):
        rd[i, i] = rt[i, i] + jnp.where(sub < 7, sroll(got[i % 4][i // 4], -1), 0.0)

    def build(i):
        even = (sub % 2 == 0)[None]
        x1r[i] = jnp.where(even, rc[:, i], rc[i])
        pm[i] = jnp.where(even, rd[i], sroll(rd[i], 1))

    each_row(build)
    level_split(pm, x1r, w1, h1, s3, c3, 1)

    def build(i):
        d = rd[i] - s3[i] - sroll(s3[i], -1)
        rd[i] = d
        fourth = (sub % 4 == 0)[None]
        pm[i] = jnp.where(fourth, sroll(d, -1), sroll(d, 1))
        x2[i] = jnp.where(fourth, c3[:, i], c3[i])

    each_row(build)
    level_split(pm, x2, w2, h2, s3, c2, 2)

    def build(i):
        d = rd[i] - sroll(s3[i], 1) - sroll(s3[i], -1)
        rd[i] = d
        pm[i] = sroll(d, 1)

    each_row(build)
    level_split(pm, c2, w3, h3, s3, None, 0)

    def build(i):
        pm[i] = rd[i] - sroll(s3[i], 3)

    each_row(build)
    inverse(pm, w4)

    back = separators(0, kept[3])
    first_sweep = backward(0, kept, back)
    zg1[z] = borders(first_sweep)
    field[...] = first_sweep
    flying = {}
    z_step(1, 0, flying)
    inside(field)
    for number in range(1, 5):
        z_step(1, number, flying)
    arriving = y_phase(1, flying)
    rhs = right_side(ghosts(1, arriving))
    kept = forward(1, rhs)
    back = separators(1, kept[3])
    out[...] = backward(1, kept, back)

    for copy in sent:
        copy.wait_send()


def body(residual, previous, edge_blocks, damping, lateral, coupling, wall_flags, wall_gain, face_table):
    def by_unknown(v):
        return jnp.transpose(v, (1, 0, 2))

    table = jnp.transpose(face_table[0])
    vmem = pl.BlockSpec(memory_space=pltpu.VMEM)
    smem = pl.BlockSpec(memory_space=pltpu.SMEM)
    far = pl.BlockSpec(memory_space=pl.ANY)
    dma = pltpu.SemaphoreType.DMA
    got = pl.pallas_call(
        kernel,
        out_shape=jax.ShapeDtypeStruct((N, 8, 256), F32),
        in_specs=[far, far, far, far, far, smem, vmem, smem, vmem, smem],
        out_specs=vmem,
        scratch_shapes=[
            pltpu.VMEM((N, 8, 256), F32),
            pltpu.VMEM((N, 8, 256), F32),
            pltpu.VMEM((N, N, 8, 256), BF16),
            pltpu.VMEM((N, 8, 256), F32),
            pltpu.VMEM((8, 4, 256), F32),
            dma((5,)),
            pltpu.VMEM((30, N, N, 8, 128), F32),
            pltpu.VMEM((N, N, 8, 128), F32),
            pltpu.VMEM((4, N, 4, 8, 128), F32),
            pltpu.VMEM((NZ, FB, 128), F32),
            pltpu.VMEM((NZ, FB, 128), F32),
            pltpu.VMEM((NY, FB, 128), F32),
            pltpu.VMEM((NY, FB, 128), F32),
            pltpu.VMEM((2, NY - 1, FB, 128), F32),
            pltpu.VMEM((NY, 8, 128), jnp.int32),
            pltpu.SMEM((NY, 8, 128), jnp.int32),
            pltpu.VMEM((512, 128), BF16),
            pltpu.VMEM((128, 1024), BF16),
            pltpu.VMEM((2, 32, 128), F32),
            pltpu.VMEM((6, 8, 256), F32),
            pltpu.VMEM((N, 8, 256), F32),
            pltpu.VMEM((N, 8, 256), F32),
            pltpu.VMEM((NLINE * MROWS, 128), F32),
            pltpu.VMEM((NLINE * MROWS, 128), F32),
            pltpu.VMEM((2, NLINE * VROWS, 128), F32),
            pltpu.VMEM((2, NLINE * VROWS, 128), F32),
            pltpu.VMEM((2, NLINE * VROWS, 128), F32),
            pltpu.VMEM((2, NLINE * VROWS, 128), F32),
            dma((2, 2, 8)),
            dma((2, 2, 8)),
            dma((2, NY - 1)),
            dma((2, NY - 1)),
            dma((NY - 1,)),
            dma((NY - 1,)),
            dma((NLINE - 1,)),
            dma((NLINE - 1,)),
            dma((2, NLINE - 1)),
            dma((2, NLINE - 1)),
            dma((2, NLINE - 1)),
            dma((2, NLINE - 1)),
            dma,
        ],
        compiler_params=pltpu.CompilerParams(
            collective_id=0, has_side_effects=True, vmem_limit_bytes=58 * 1024 * 1024
        ),
        name="line_sweeps",
    )(
        by_unknown(residual),
        by_unknown(previous),
        jnp.transpose(edge_blocks, (1, 2, 0, 3)),
        by_unknown(damping),
        lateral,
        coupling,
        wall_flags.reshape(1, 256),
        wall_gain,
        table,
        table,
    )
    return jnp.transpose(got, (1, 0, 2))


def solution(mesh):
    placed = (
        P("line", None, "surf"),
        P("line", None, "surf"),
        P("line", None, None, "surf"),
        P("line", None, "surf"),
        P("line", None, "surf"),
        P(),
        P("surf"),
        P(),
        P("surf", None, None),
    )
    return jax.shard_map(
        body, mesh=mesh, in_specs=placed, out_specs=P("line", None, "surf"), check_vma=False
    )
```

```python
import functools

import jax
import jax.numpy as jnp
from jax import lax
from jax.experimental import pallas as pl
from jax.experimental.pallas import tpu as pltpu
from jax.sharding import PartitionSpec as P

N = 13
PW = 16
NY = 4
NZ = 16
NLINE = 8
FB = 56
MROWS = 96
VROWS = 8
MESH = pl.DeviceIdType.MESH
F32 = jnp.float32
BF16 = jnp.bfloat16


def sub_of(shape):
    return lax.broadcasted_iota(jnp.int32, shape, len(shape) - 2)


def lane_of(shape):
    return lax.broadcasted_iota(jnp.int32, shape, len(shape) - 1)


def sroll(x, k):
    return pltpu.roll(x, k % 8, x.ndim - 2)


def lroll(x, k):
    return pltpu.roll(x, k % x.shape[-1], x.ndim - 1)


def mm(out, a, b, ta=False):
    def rows(at):
        acc = [None] * len(at)
        for k in range(N):
            bk = b[k]
            for n, i in enumerate(at):
                term = (a[k, i] if ta else a[i, k])[None] * bk
                acc[n] = term if k == 0 else acc[n] + term
        for n, i in enumerate(at):
            out[i] = acc[n]

    def pair(q, carry):
        rows([2 * q, 2 * q + 1])
        return carry

    lax.fori_loop(0, N // 2, pair, 0)
    rows([N - 1])


def mm_upper(out, a, b):
    for top in range(0, N, 2):
        at = [i for i in (top, top + 1) if i < N]
        acc = [None] * len(at)
        for k in range(N):
            bk = b[k, pl.ds(top, N - top)]
            for n, i in enumerate(at):
                term = a[k, i][None] * bk
                acc[n] = term if k == 0 else acc[n] + term
        for n, i in enumerate(at):
            out[i, pl.ds(top, N - top)] = acc[n]


def mm_split(out, a, b, ta=False, shift=0, upper=False):
    for at in (range(0, 4), range(4, 8), range(8, N)):
        low = at[0] // 4 if upper else 0
        acc = [None] * len(at)
        for k in range(N):
            bk = b[k, pl.ds(low, 4 - low)]
            if shift:
                bk = sroll(bk, -shift)
            for n, i in enumerate(at):
                term = (a[k, i] if ta else a[i, k])[None] * bk
                acc[n] = term if k == 0 else acc[n] + term
        for n, i in enumerate(at):
            out[i, pl.ds(low, 4 - low)] = acc[n]


def spread_groups(v):
    turns = [v] + [lroll(v, 32 * k) for k in range(1, 4)]
    quarter = (lane_of((8, 128)) // 32)[None]
    got = []
    for g in range(4):
        x = turns[3]
        for k in range(3):
            x = jnp.where(quarter == (g + k) % 4, turns[k], x)
        got.append(x)
    return got


def inverse(src, dst):
    a = [src[i, pl.ds(i, N - i)] for i in range(N)]
    for p in range(N):
        d = 1.0 / a[p][0:1]
        parts = [a[i][p - i : p - i + 1] for i in range(p)] + [a[p]]
        col = jnp.concatenate(parts, axis=0) if p else a[p]
        scaled = col * d
        for i in range(N):
            if i == p:
                continue
            new = a[i] - col[i : i + 1] * scaled[i:]
            if i < p:
                pieces = [new[: p - i], scaled[i : i + 1]]
                if p - i + 1 < N - i:
                    pieces.append(new[p - i + 1 :])
                new = jnp.concatenate(pieces, axis=0)
            a[i] = new
        a[p] = jnp.concatenate([-d, scaled[p + 1 :]], axis=0) if p + 1 < N else -d
    for i in range(N):
        neg = -a[i]
        dst[i, pl.ds(i, N - i)] = neg
        for j in range(i + 1, N):
            dst[j, i] = neg[j - i]


def mvt(g, x):
    acc = x[0:1] * g[0]
    for k in range(1, N):
        acc = acc + x[k : k + 1] * g[k]
    return acc


def mv(g, x):
    acc = x[0:1] * g[:, 0]
    for k in range(1, N):
        acc = acc + x[k : k + 1] * g[:, k]
    return acc


def exchange_groups(v):
    which = (lane_of((8, 128)) // 32 - sub_of((8, 128)) // 2 + 4) % 4
    out = v
    for step in range(1, 4):
        out = jnp.where((which == step)[None], sroll(lroll(v, 32 * step), -2 * step), out)
    return out


def split_cells(v):
    h0, h1 = v[:, :, :128], v[:, :, 128:]
    even = (sub_of((8, 128)) % 2 == 0)[None]
    return jnp.where(even, h0, sroll(h1, 1)), jnp.where(even, sroll(h0, -1), h1)


def join_cells(xe, xo):
    even = (sub_of((8, 128)) % 2 == 0)[None]
    h0 = jnp.where(even, xe, sroll(xo, 1))
    h1 = jnp.where(even, sroll(xe, -1), xo)
    return jnp.concatenate([h0, h1], axis=2)


def three_parts(x):
    high = x.astype(BF16).astype(F32)
    rest = x - high
    mid = rest.astype(BF16).astype(F32)
    return jnp.concatenate([high, mid, rest - mid], axis=0).astype(BF16)


def kernel(
    res_any, prev_any, edge_any, damp_any, lat_any, coup, flags, gain, tab_v, tab_s, out,
    res, prev, edge, damp, lat, ins, mats, work, thin, zg0, zg1, yb0, yb1, ysend, tscr, tsm, pick, spread, lsc, wts, inner, field,
    fs, fr, vs, vr, bs, br,
    zss, zrs, yss, yrs, tss, trs, fss, frs, vss, vrs, bss, brs, lsem,
):
    zgs, ybs = (zg0, zg1), (yb0, yb1)
    place = lax.axis_index("line")
    patch = lax.axis_index("surf")
    z, y = patch // NY, patch % NY

    def line_dev(k):
        return (lax.rem(place + k, NLINE), patch)

    def z_dev(k):
        return (place, lax.rem(z + k + NZ, NZ) * NY + y)

    def y_dev(k):
        return (place, z * NY + lax.rem(y + k, NY))

    barrier = pltpu.get_barrier_semaphore()
    friends = [z_dev(k) for k in (4, -4, 3, -3, 2, -2, 1, -1)]
    friends += [line_dev(k) for k in (4, 3, 5, 2, 6, 1, 7)]
    friends += [y_dev(k) for k in (2, 1, 3)]
    for friend in friends:
        pl.semaphore_signal(barrier, inc=1, device_id=friend, device_id_type=MESH)

    loads = {}
    pairs = dict(prev=(prev_any, prev), edge=(edge_any, edge), damp=(damp_any, damp), lat=(lat_any, lat), res=(res_any, res))
    for n, (name, (far, near)) in enumerate(pairs.items()):
        loads[name] = pltpu.make_async_copy(far, near, ins.at[n])
        loads[name].start()

    sent = []

    def send(src, dst, ssem, rsem, target):
        copy = pltpu.make_async_remote_copy(
            src_ref=src, dst_ref=dst, send_sem=ssem, recv_sem=rsem, device_id=target, device_id_type=MESH
        )
        copy.start()
        sent.append(copy)
        return copy

    def settle(count):
        while len(sent) > count:
            sent.pop(0).wait_send()

    tile = (8, 128)
    sub, lane = sub_of(tile), lane_of(tile)
    slot = sub // 2

    line = lax.broadcasted_iota(jnp.int32, (512, 128), 0)
    col = lax.broadcasted_iota(jnp.int32, (512, 128), 1)
    face, pos = (col // 16) % 4, col % 16
    row_at, col_at = (line % 256) // PW, line % PW
    across = jnp.where(face < 2, row_at, col_at)
    along = jnp.where(face < 2, col_at, row_at)
    hit = (across == (face % 2) * (PW - 1)) & (along == pos) & (line // 256 == col // 64)
    pick[...] = jnp.where(hit, 1.0, 0.0).astype(BF16)

    def borders(values):
        low = values[0:7].reshape(FB, 256)
        high = jnp.concatenate([values[7:N], jnp.zeros((1, 8, 256), F32)], axis=0).reshape(FB, 256)
        wide = jnp.concatenate([low, high], axis=1)
        got = jnp.dot(three_parts(wide), pick[...], preferred_element_type=F32)
        return got[0:FB] + got[FB : 2 * FB] + got[2 * FB :]

    def z_send(ph, d, dist, hop):
        step = 1 - 2 * lax.rem(z, 2) if d == 0 else d
        at = lax.rem(z - step * (dist - hop) + NZ, NZ)
        return send(
            zgs[ph].at[at], zgs[ph].at[at], zss.at[ph, d + 1, dist - 1], zrs.at[ph, d + 1, dist - 1], z_dev(step * hop)
        )

    def z_step(ph, number, flying):
        waited, plan = (
            (0, ((4, 4), (1, 1))),
            (1, ((3, 2), (2, 1))),
            (4, ((8, 4), (7, 3), (6, 2), (5, 1))),
        )[number]
        if waited:
            for d in (1, -1):
                flying.pop((d, waited)).wait_recv()
        for dist, hop in plan:
            for d in (0,) if dist == 8 else (1, -1):
                flying[(d, dist)] = z_send(ph, d, dist, hop)

    group = (lane_of((FB, 128)) // 16) % 4

    def choose(blocks):
        got = jnp.where(group == 1, blocks[0], jnp.where(group == 0, blocks[1], jnp.where(group == 3, blocks[2], blocks[3])))
        return got

    def y_phase(ph, flying):
        for copy in flying.values():
            copy.wait_recv()
        arriving = []
        for k in (2, 1, 3, 0):
            to = lax.rem(y + k, NY)
            block = choose([zgs[ph][tsm[to, 0, f] // NY] for f in range(4)])
            if k == 0:
                ybs[ph][y] = block
            else:
                ysend[ph, k - 1] = block
                arriving.append(
                    send(ysend.at[ph, k - 1], ybs[ph].at[y], yss.at[ph, k - 1], yrs.at[ph, k - 1], y_dev(k))
                )
        return arriving

    def ghosts(ph, arriving):
        for copy in arriving:
            copy.wait_recv()
        block = choose([ybs[ph][tsm[y, 0, f] % NY] for f in range(4)])
        got = jnp.dot(three_parts(block), spread[...], preferred_element_type=F32)
        got = got[0:FB] + got[FB : 2 * FB] + got[2 * FB :]
        return got

    def all_to_all(src, dst, rows, ssem, rsem):
        own = pl.multiple_of(place * rows, 8)
        arriving = []
        for k in (4, 3, 5, 2, 6, 1, 7):
            to = pl.multiple_of(lax.rem(place + k, NLINE) * rows, 8)
            arriving.append(
                send(src.at[pl.ds(to, rows)], dst.at[pl.ds(own, rows)], ssem.at[k - 1], rsem.at[k - 1], line_dev(k))
            )
        dst[pl.ds(own, rows)] = src[pl.ds(own, rows)]
        return arriving

    loads["prev"].wait()
    zg0[z] = borders(prev[...])
    tscr[y] = jnp.zeros(tile, jnp.int32)
    tscr[y, 0:2, 0:4] = tab_v[...]
    pl.semaphore_wait(barrier, len(friends))
    flying = {}
    z_step(0, 0, flying)
    tables = [send(tscr.at[y], tscr.at[y], tss.at[k - 1], trs.at[k - 1], y_dev(k)) for k in range(1, NY)]

    (uo, ue, pm, dd, v1, gl, gr, c1, sl, sr, x2, v2, g2, s2, c2, x3, v3, g3, s3, c3, rc, rd,
     w1, h1, x1r, w2, h2, w3, h3, w4) = [mats.at[n] for n in range(30)]

    def each_row(body):
        def step(i, carry):
            body(i)
            return carry

        lax.fori_loop(0, N, step, 0, unroll=True)

    first = ((sub < 2) & (place == 0))[None]
    even_sub = (sub % 2 == 0)[None]

    def build(i):
        e = edge[i].astype(F32)
        h0, h1 = e[:, :, :128], e[:, :, 128:]
        u = jnp.where(even_sub, h0, sroll(h1, 1))
        o = jnp.where(even_sub, sroll(h0, -1), h1)
        uo[i] = o
        ue[i] = jnp.where(first, 0.0, u)
        pm[i] = u + o
        dd[i] = o + jnp.where((sub < 6)[None], sroll(u, -2), 0.0)

    loads["edge"].wait()
    each_row(build)
    loads["damp"].wait()
    de, do = split_cells(damp[...])
    flag = flags[...].astype(F32)
    wall = jnp.where(sub == 0, flag[:, :128], flag[:, 128:])
    wall = jnp.where(first[0], wall, 0.0)
    for i in range(N):
        pm[i, i] = pm[i, i] + de[i] + wall * gain[i]
        dd[i, i] = dd[i, i] + do[i]
    inverse(pm, v1)
    mm(gl, v1, ue)
    mm(gr, v1, uo)
    z_step(0, 1, flying)
    mm_upper(sl, ue, gl)
    mm_upper(sr, uo, gr)
    mm(c1, ue, gr)

    def level(p, x, v, g, s, c, shift, between):
        inverse(p, v)
        mm(g, v, x)
        between()
        mm_upper(s, x, g)

        def turn(i):
            work[i] = sroll(g[i], -shift)

        each_row(turn)
        mm(c, x, work, True)

    def level_split(p, x, v, g, s, c, shift):
        inverse(p, v)
        xs, gs, ss, cs = [thin.at[n] for n in range(4)]
        quarter = lane // 32

        def split(k):
            for q in range(4):
                got = x[k, 4 * q]
                for n in range(1, min(4, N - 4 * q)):
                    got = jnp.where(quarter == n, x[k, 4 * q + n], got)
                xs[k, q] = got

        each_row(split)
        mm_split(gs, v, xs)
        mm_split(ss, x, gs, True, upper=True)
        if c is not None:
            mm_split(cs, x, gs, True, shift)

        def join(i):
            for q in range(4):
                wide = min(4, N - 4 * q)
                full = spread_groups(ss[i, q][None])
                far = spread_groups(cs[i, q][None]) if c is not None else None
                for n in range(wide):
                    g[i, 4 * q + n] = lroll(gs[i, q], -32 * n) if n else gs[i, q]
                    s[i, 4 * q + n] = full[n][0]
                    if c is not None:
                        c[i, 4 * q + n] = far[n][0]

        each_row(join)

    def build(i):
        d = dd[i] - sr[i] - jnp.where((sub < 6)[None], sroll(sl[i], -2), 0.0)
        dd[i] = d
        even = (slot % 2 == 0)[None]
        pm[i] = jnp.where(even, d, sroll(d, 2))
        x2[i] = jnp.where(even, c1[:, i], c1[i])

    each_row(build)
    level(pm, x2, v2, g2, s2, c2, 2, lambda: z_step(0, 2, flying))
    for copy in tables:
        copy.wait_recv()
    to_smem = pltpu.make_async_copy(tscr, tsm, lsem)
    to_smem.start()

    def build(i):
        d = dd[i] - s2[i] - jnp.where((slot == 1)[None], sroll(s2[i], -2), 0.0)
        dd[i] = d
        low = (slot == 0)[None]
        pm[i] = jnp.where(low, sroll(d, -2), sroll(d, 2))
        x3[i] = jnp.where(low, c2[:, i], c2[i])

    each_row(build)
    level(pm, x3, v3, g3, s3, c3, 4, lambda: None)

    def build(i):
        own = dd[i] - sroll(s3[i], 2)
        push = ue[:, i] - sl[:, i] - s2[:, i] - s3[:, i]
        cross = c3[i]
        rows = []
        for q in range(7):
            j = 2 * q
            parts = [cross[j], jnp.where(j >= i, sroll(own[j], 4), sroll(push[j], 2))]
            if j + 1 < N:
                parts += [sroll(cross[j + 1], 4), jnp.where(j + 1 >= i, own[j + 1], sroll(push[j + 1], -2))]
            else:
                parts += [jnp.zeros(tile, F32)] * 2
            v = parts[3]
            for t in range(3):
                v = jnp.where(slot == t, parts[t], v)
            rows.append(v[None])
        v = exchange_groups(jnp.concatenate(rows, axis=0))
        for q in range(7):
            fs[pl.ds(i * 7 + q, 8, stride=MROWS), :] = v[q]

    each_row(build)
    rows = []
    for q in range(4):
        v = jnp.zeros(tile, F32)
        for t in range(min(4, N - 4 * q)):
            i = 4 * q + t
            v = jnp.where(slot == t, sroll(ue[i, i] - sl[i, i] - s2[i, i] - s3[i, i], 2 * t), v)
        rows.append(v[None])
    v = exchange_groups(jnp.concatenate(rows, axis=0))
    for q in range(4):
        fs[pl.ds(91 + q, 8, stride=MROWS), :] = v[q]
    fs[pl.ds(95, 8, stride=MROWS), :] = jnp.zeros(tile, F32)
    blocks = all_to_all(fs, fr, MROWS, fss, frs)

    to_smem.wait()
    arriving = y_phase(0, flying)

    src = lax.broadcasted_iota(jnp.int32, (128, 1024), 0)
    dst = lax.broadcasted_iota(jnp.int32, (128, 1024), 1)
    face = ((src // 16) % 4) ^ 1
    turned = jnp.where(face == 0, tab_s[1, 0], jnp.where(face == 1, tab_s[1, 1], jnp.where(face == 2, tab_s[1, 2], tab_s[1, 3])))
    line = dst % 256
    across = jnp.where(face < 2, line // PW, line % PW)
    along = jnp.where(face < 2, line % PW, line // PW)
    along = along + turned * (PW - 1 - 2 * along)
    hit = (across == (face % 2) * (PW - 1)) & (along == src % 16)
    hit = hit & (dst // 512 == src // 64) & ((dst // 256) % 2 == face // 2)
    spread[...] = jnp.where(hit, 1.0, 0.0).astype(BF16)

    loads["lat"].wait()
    loads["res"].wait()
    for c in range(8):
        for h in range(2):
            lsc[h, pl.ds(4 * c, 4), :] = lat[c, :, pl.ds(128 * h, 128)]
    lats = [
        jnp.concatenate([lsc[h, pl.ds(d, 8, stride=4), :] for h in range(2)], axis=1) for d in range(4)
    ]
    line = lane_of((8, 256))
    edges = [line < PW, line >= 256 - PW, line % PW == 0, line % PW == PW - 1]
    for d in range(4):
        wts[d] = jnp.where(edges[d], 0.0, lats[d])
    for kind in range(2):
        wts[4 + kind] = jnp.where(
            edges[2 * kind], lats[2 * kind], jnp.where(edges[2 * kind + 1], lats[2 * kind + 1], 0.0)
        )

    def inside(v):
        for i in range(N):
            x = v[i]
            inner[i] = (
                wts[0] * lroll(x, PW) + wts[1] * lroll(x, -PW) + wts[2] * lroll(x, 1) + wts[3] * lroll(x, -1)
            )

    def right_side(got):
        weighted = []
        for i in range(N):
            at, base = (8 * i, 0) if i < 7 else (8 * (i - 7), 512)
            weighted.append(
                inner[i] + wts[4] * got[at : at + 8, base : base + 256] + wts[5] * got[at : at + 8, base + 256 : base + 512]
            )
        rows = []
        for a in range(N):
            acc = res[a]
            for b in range(N):
                acc = acc - coup[a, b] * weighted[b]
            rows.append(acc[None])
        return jnp.concatenate(rows, axis=0)

    def forward(ph, rhs):
        re, ro = split_cells(rhs)
        ul, ur = mvt(gl, re), mvt(gr, re)
        ro = ro + ur + jnp.where((sub < 6)[None], sroll(ul, -2), 0.0)
        rk2 = jnp.where((slot % 2 == 0)[None], ro, sroll(ro, 2))
        u2 = mvt(g2, rk2)
        ro = ro + u2 + jnp.where((slot == 1)[None], sroll(u2, -2), 0.0)
        rk3 = jnp.where((slot == 0)[None], sroll(ro, -2), sroll(ro, 2))
        u3 = mvt(g3, rk3)
        own = ro + sroll(u3, 2)
        tip = ul + u2 + u3
        rows = []
        for q in range(7):
            j = 2 * q
            v = jnp.where(slot == 0, tip[j], jnp.where(slot == 1, sroll(own[j], 4), 0.0))
            if j + 1 < N:
                v = jnp.where(slot == 2, sroll(tip[j + 1], 4), jnp.where(slot == 3, own[j + 1], v))
            rows.append(v[None])
        v = exchange_groups(jnp.concatenate(rows, axis=0))
        for q in range(7):
            vs[ph, pl.ds(q, 8, stride=VROWS), :] = v[q]
        vs[ph, pl.ds(7, 8, stride=VROWS), :] = jnp.zeros(tile, F32)
        arriving = all_to_all(vs.at[ph], vr.at[ph], VROWS, vss.at[ph], vrs.at[ph])
        return re, rk2, rk3, arriving

    def separators(ph, arriving):
        for copy in arriving:
            copy.wait_recv()
        got = [vr[ph, pl.ds(q, 8, stride=VROWS), :] for q in range(7)]
        tips = jnp.concatenate([(lroll(got[j // 2], 64) if j % 2 else got[j // 2])[None] for j in range(N)], axis=0)
        owns = jnp.concatenate([lroll(got[j // 2], 32 if j % 2 else 96)[None] for j in range(N)], axis=0)
        r = owns + jnp.where((sub < 7)[None], sroll(tips, -1), 0.0)
        even = (sub % 2 == 0)[None]
        fourth = (sub % 4 == 0)[None]
        rk1 = jnp.where(even, r, sroll(r, 1))
        u = mvt(h1, rk1)
        r = r + u + sroll(u, -1)
        rk2 = jnp.where(fourth, sroll(r, -1), sroll(r, 1))
        u = mvt(h2, rk2)
        r = r + sroll(u, 1) + sroll(u, -1)
        rk3 = sroll(r, 1)
        u = mvt(h3, rk3)
        x7 = mvt(w4, r + sroll(u, 3))
        x3 = sroll(mvt(w3, rk3) + mv(h3, sroll(x7, -3)), -1)
        known = jnp.where((sub == 3)[None], x3, x7)
        near = jnp.where((sub == 2)[None], sroll(x3, -1), jnp.where((sub == 4)[None], sroll(x3, 1), sroll(x7, -1)))
        near = jnp.where((sub == 0)[None], 0.0, near)
        u = mv(h2, near) + jnp.where(fourth, mvt(w2, rk2), 0.0)
        x = jnp.where((sub % 4 == 1)[None], sroll(u, 1) + sroll(u, -1), known)
        near = jnp.where((sub == 0)[None], 0.0, jnp.where(even, sroll(x, 1), x))
        u = mv(h1, near) + jnp.where(even, mvt(w1, rk1), 0.0)
        x = jnp.where(even, u + sroll(u, -1), x)
        below = jnp.where((sub == 0)[None], 0.0, sroll(x, 1))
        quarter = lane // 32
        for q in range(7):
            j = 2 * q
            v = jnp.where(quarter == 0, below[j], jnp.where(quarter == 1, lroll(x[j], 32), 0.0))
            if j + 1 < N:
                v = jnp.where(quarter == 2, lroll(below[j + 1], 64), jnp.where(quarter == 3, lroll(x[j + 1], 96), v))
            bs[ph, pl.ds(q, 8, stride=VROWS), :] = v
        bs[ph, pl.ds(7, 8, stride=VROWS), :] = jnp.zeros(tile, F32)
        return all_to_all(bs.at[ph], br.at[ph], VROWS, bss.at[ph], brs.at[ph])

    def backward(ph, kept, arriving):
        re, rk2, rk3, _ = kept
        y1, y2, y3 = mvt(v1, re), mvt(v2, rk2), mvt(v3, rk3)
        for copy in arriving:
            copy.wait_recv()
        got = jnp.concatenate([br[ph, pl.ds(q, 8, stride=VROWS), :][None] for q in range(7)], axis=0)
        got = exchange_groups(got)
        ends = []
        for j in range(N):
            v = got[j // 2]
            low, mid, top = (sroll(v, 4), sroll(v, -2), v) if j % 2 else (v, sroll(v, 2), sroll(v, 4))
            ends.append(jnp.where(slot == 0, low, jnp.where(slot == 2, mid, jnp.where(slot == 3, top, 0.0)))[None])
        ends = jnp.concatenate(ends, axis=0)
        u = mv(g3, ends) + jnp.where((slot == 0)[None], y3, 0.0)
        x3 = sroll(u, 2) + sroll(u, -2)
        near = jnp.where((slot == 1)[None], x3, jnp.where((slot == 2)[None], sroll(x3, 2), ends))
        u = mv(g2, near) + jnp.where((slot % 2 == 0)[None], y2, 0.0)
        both = u + sroll(u, -2)
        xo = jnp.where((slot % 2 == 0)[None], both, jnp.where((slot == 1)[None], x3, ends))
        xl = jnp.where((slot == 0)[None], ends, sroll(xo, 2))
        xe = y1 + mv(gl, xl) + mv(gr, xo)
        return join_cells(xe, xo)

    inside(prev)
    rhs = right_side(ghosts(0, arriving))
    kept = forward(0, rhs)

    rt = sr
    for copy in blocks:
        copy.wait_recv()

    def build(i):
        rows = [fr[pl.ds(i * 7 + q, 8, stride=MROWS), :][None] for q in range(7)]
        got = spread_groups(jnp.concatenate(rows, axis=0))
        for j in range(N):
            rc[i, j] = got[j % 2 * 2][j // 2]
            rt[i, j] = got[j % 2 * 2 + 1][j // 2]

    each_row(build)

    def build(i):
        rd[i] = rt[i] + jnp.where((sub < 7)[None], sroll(rt[:, i], -1), 0.0)

    each_row(build)
    rows = [fr[pl.ds(91 + q, 8, stride=MROWS), :][None] for q in range(4)]
    got = spread_groups(jnp.concatenate(rows, axis=0))
    for i in range(N):
        rd[i, i] = rt[i, i] + jnp.where(sub < 7, sroll(got[i % 4][i // 4], -1), 0.0)

    def build(i):
        even = (sub % 2 == 0)[None]
        x1r[i] = jnp.where(even, rc[:, i], rc[i])
        pm[i] = jnp.where(even, rd[i], sroll(rd[i], 1))

    each_row(build)
    level_split(pm, x1r, w1, h1, s3, c3, 1)

    def build(i):
        d = rd[i] - s3[i] - sroll(s3[i], -1)
        rd[i] = d
        fourth = (sub % 4 == 0)[None]
        pm[i] = jnp.where(fourth, sroll(d, -1), sroll(d, 1))
        x2[i] = jnp.where(fourth, c3[:, i], c3[i])

    each_row(build)
    level_split(pm, x2, w2, h2, s3, c2, 2)

    def build(i):
        d = rd[i] - sroll(s3[i], 1) - sroll(s3[i], -1)
        rd[i] = d
        pm[i] = sroll(d, 1)

    each_row(build)
    level_split(pm, c2, w3, h3, s3, None, 0)

    def build(i):
        pm[i] = rd[i] - sroll(s3[i], 3)

    each_row(build)
    inverse(pm, w4)

    back = separators(0, kept[3])
    first_sweep = backward(0, kept, back)
    zg1[z] = borders(first_sweep)
    field[...] = first_sweep
    flying = {}
    z_step(1, 0, flying)
    inside(field)
    settle(4)
    for number in (1, 2):
        z_step(1, number, flying)
    arriving = y_phase(1, flying)
    settle(3)
    rhs = right_side(ghosts(1, arriving))
    kept = forward(1, rhs)
    settle(7)
    back = separators(1, kept[3])
    settle(7)
    out[...] = backward(1, kept, back)

    settle(0)


def body(residual, previous, edge_blocks, damping, lateral, coupling, wall_flags, wall_gain, face_table):
    def by_unknown(v):
        return jnp.transpose(v, (1, 0, 2))

    table = jnp.transpose(face_table[0])
    vmem = pl.BlockSpec(memory_space=pltpu.VMEM)
    smem = pl.BlockSpec(memory_space=pltpu.SMEM)
    far = pl.BlockSpec(memory_space=pl.ANY)
    dma = pltpu.SemaphoreType.DMA
    got = pl.pallas_call(
        kernel,
        out_shape=jax.ShapeDtypeStruct((N, 8, 256), F32),
        in_specs=[far, far, far, far, far, smem, vmem, smem, vmem, smem],
        out_specs=vmem,
        scratch_shapes=[
            pltpu.VMEM((N, 8, 256), F32),
            pltpu.VMEM((N, 8, 256), F32),
            pltpu.VMEM((N, N, 8, 256), BF16),
            pltpu.VMEM((N, 8, 256), F32),
            pltpu.VMEM((8, 4, 256), F32),
            dma((5,)),
            pltpu.VMEM((30, N, N, 8, 128), F32),
            pltpu.VMEM((N, N, 8, 128), F32),
            pltpu.VMEM((4, N, 4, 8, 128), F32),
            pltpu.VMEM((NZ, FB, 128), F32),
            pltpu.VMEM((NZ, FB, 128), F32),
            pltpu.VMEM((NY, FB, 128), F32),
            pltpu.VMEM((NY, FB, 128), F32),
            pltpu.VMEM((2, NY - 1, FB, 128), F32),
            pltpu.VMEM((NY, 8, 128), jnp.int32),
            pltpu.SMEM((NY, 8, 128), jnp.int32),
            pltpu.VMEM((512, 128), BF16),
            pltpu.VMEM((128, 1024), BF16),
            pltpu.VMEM((2, 32, 128), F32),
            pltpu.VMEM((6, 8, 256), F32),
            pltpu.VMEM((N, 8, 256), F32),
            pltpu.VMEM((N, 8, 256), F32),
            pltpu.VMEM((NLINE * MROWS, 128), F32),
            pltpu.VMEM((NLINE * MROWS, 128), F32),
            pltpu.VMEM((2, NLINE * VROWS, 128), F32),
            pltpu.VMEM((2, NLINE * VROWS, 128), F32),
            pltpu.VMEM((2, NLINE * VROWS, 128), F32),
            pltpu.VMEM((2, NLINE * VROWS, 128), F32),
            dma((2, 3, 8)),
            dma((2, 3, 8)),
            dma((2, NY - 1)),
            dma((2, NY - 1)),
            dma((NY - 1,)),
            dma((NY - 1,)),
            dma((NLINE - 1,)),
            dma((NLINE - 1,)),
            dma((2, NLINE - 1)),
            dma((2, NLINE - 1)),
            dma((2, NLINE - 1)),
            dma((2, NLINE - 1)),
            dma,
        ],
        compiler_params=pltpu.CompilerParams(
            collective_id=0, has_side_effects=True, vmem_limit_bytes=58 * 1024 * 1024
        ),
        name="line_sweeps",
    )(
        by_unknown(residual),
        by_unknown(previous),
        jnp.transpose(edge_blocks, (1, 2, 0, 3)),
        by_unknown(damping),
        lateral,
        coupling,
        wall_flags.reshape(1, 256),
        wall_gain,
        table,
        table,
    )
    return jnp.transpose(got, (1, 0, 2))


def solution(mesh):
    placed = (
        P("line", None, "surf"),
        P("line", None, "surf"),
        P("line", None, None, "surf"),
        P("line", None, "surf"),
        P("line", None, "surf"),
        P(),
        P("surf"),
        P(),
        P("surf", None, None),
    )
    return jax.shard_map(
        body, mesh=mesh, in_specs=placed, out_specs=P("line", None, "surf"), check_vma=False
    )
```

```python
import functools

import jax
import jax.numpy as jnp
from jax import lax
from jax.experimental import pallas as pl
from jax.experimental.pallas import tpu as pltpu
from jax.sharding import PartitionSpec as P

N = 13
PW = 16
NY = 4
NZ = 16
NLINE = 8
FB = 56
MROWS = 96
VROWS = 8
MESH = pl.DeviceIdType.MESH
F32 = jnp.float32
BF16 = jnp.bfloat16


def sub_of(shape):
    return lax.broadcasted_iota(jnp.int32, shape, len(shape) - 2)


def lane_of(shape):
    return lax.broadcasted_iota(jnp.int32, shape, len(shape) - 1)


def sroll(x, k):
    return pltpu.roll(x, k % 8, x.ndim - 2)


def lroll(x, k):
    return pltpu.roll(x, k % x.shape[-1], x.ndim - 1)


def mm(out, a, b, ta=False):
    def rows(at):
        acc = [None] * len(at)
        for k in range(N):
            bk = b[k]
            for n, i in enumerate(at):
                term = (a[k, i] if ta else a[i, k])[None] * bk
                acc[n] = term if k == 0 else acc[n] + term
        for n, i in enumerate(at):
            out[i] = acc[n]

    def pair(q, carry):
        rows([2 * q, 2 * q + 1])
        return carry

    lax.fori_loop(0, N // 2, pair, 0)
    rows([N - 1])


def mm_upper(out, a, b):
    for top in range(0, N, 2):
        at = [i for i in (top, top + 1) if i < N]
        acc = [None] * len(at)
        for k in range(N):
            bk = b[k, pl.ds(top, N - top)]
            for n, i in enumerate(at):
                term = a[k, i][None] * bk
                acc[n] = term if k == 0 else acc[n] + term
        for n, i in enumerate(at):
            out[i, pl.ds(top, N - top)] = acc[n]


def mm_split(out, a, b, ta=False, shift=0, upper=False):
    for at in (range(0, 4), range(4, 8), range(8, N)):
        low = at[0] // 4 if upper else 0
        acc = [None] * len(at)
        for k in range(N):
            bk = b[k, pl.ds(low, 4 - low)]
            if shift:
                bk = sroll(bk, -shift)
            for n, i in enumerate(at):
                term = (a[k, i] if ta else a[i, k])[None] * bk
                acc[n] = term if k == 0 else acc[n] + term
        for n, i in enumerate(at):
            out[i, pl.ds(low, 4 - low)] = acc[n]


def spread_groups(v):
    turns = [v] + [lroll(v, 32 * k) for k in range(1, 4)]
    quarter = (lane_of((8, 128)) // 32)[None]
    got = []
    for g in range(4):
        x = turns[3]
        for k in range(3):
            x = jnp.where(quarter == (g + k) % 4, turns[k], x)
        got.append(x)
    return got


def inverse(src, dst):
    a = [src[i, pl.ds(i, N - i)] for i in range(N)]
    for p in range(N):
        d = 1.0 / a[p][0:1]
        parts = [a[i][p - i : p - i + 1] for i in range(p)] + [a[p]]
        col = jnp.concatenate(parts, axis=0) if p else a[p]
        scaled = col * d
        for i in range(N):
            if i == p:
                continue
            new = a[i] - col[i : i + 1] * scaled[i:]
            if i < p:
                pieces = [new[: p - i], scaled[i : i + 1]]
                if p - i + 1 < N - i:
                    pieces.append(new[p - i + 1 :])
                new = jnp.concatenate(pieces, axis=0)
            a[i] = new
        a[p] = jnp.concatenate([-d, scaled[p + 1 :]], axis=0) if p + 1 < N else -d
    for i in range(N):
        neg = -a[i]
        dst[i, pl.ds(i, N - i)] = neg
        for j in range(i + 1, N):
            dst[j, i] = neg[j - i]


def mvt(g, x):
    acc = x[0:1] * g[0]
    for k in range(1, N):
        acc = acc + x[k : k + 1] * g[k]
    return acc


def mv(g, x):
    acc = x[0:1] * g[:, 0]
    for k in range(1, N):
        acc = acc + x[k : k + 1] * g[:, k]
    return acc


def exchange_groups(v):
    which = (lane_of((8, 128)) // 32 - sub_of((8, 128)) // 2 + 4) % 4
    out = v
    for step in range(1, 4):
        out = jnp.where((which == step)[None], sroll(lroll(v, 32 * step), -2 * step), out)
    return out


def split_cells(v):
    h0, h1 = v[:, :, :128], v[:, :, 128:]
    even = (sub_of((8, 128)) % 2 == 0)[None]
    return jnp.where(even, h0, sroll(h1, 1)), jnp.where(even, sroll(h0, -1), h1)


def join_cells(xe, xo):
    even = (sub_of((8, 128)) % 2 == 0)[None]
    h0 = jnp.where(even, xe, sroll(xo, 1))
    h1 = jnp.where(even, sroll(xe, -1), xo)
    return jnp.concatenate([h0, h1], axis=2)


def three_parts(x):
    high = x.astype(BF16).astype(F32)
    rest = x - high
    mid = rest.astype(BF16).astype(F32)
    return jnp.concatenate([high, mid, rest - mid], axis=0).astype(BF16)


def kernel(
    res_any, prev_any, edge_any, damp_any, lat_any, coup, flags, gain, tab_v, tab_s, out,
    res, prev, edge, damp, lat, ins, mats, work, thin, zg0, zg1, yb0, yb1, ysend, tscr, tsm, pick, spread, lsc, wts, inner, field,
    fs, fr, vs, vr, bs, br,
    zss, zrs, yss, yrs, tss, trs, fss, frs, vss, vrs, bss, brs, lsem,
):
    zgs, ybs = (zg0, zg1), (yb0, yb1)
    place = lax.axis_index("line")
    patch = lax.axis_index("surf")
    z, y = patch // NY, patch % NY

    def line_dev(k):
        return (lax.rem(place + k, NLINE), patch)

    def z_dev(k):
        return (place, lax.rem(z + k + NZ, NZ) * NY + y)

    def y_dev(k):
        return (place, z * NY + lax.rem(y + k, NY))

    barrier = pltpu.get_barrier_semaphore()
    friends = [z_dev(k) for k in (4, -4, 3, -3, 2, -2, 1, -1)]
    friends += [line_dev(k) for k in (4, 3, 5, 2, 6, 1, 7)]
    friends += [y_dev(k) for k in (2, 1, 3)]
    for friend in friends:
        pl.semaphore_signal(barrier, inc=1, device_id=friend, device_id_type=MESH)

    loads = {}
    pairs = dict(prev=(prev_any, prev), edge=(edge_any, edge), damp=(damp_any, damp), lat=(lat_any, lat), res=(res_any, res))
    for n, (name, (far, near)) in enumerate(pairs.items()):
        loads[name] = pltpu.make_async_copy(far, near, ins.at[n])
        loads[name].start()

    sent = []

    def send(src, dst, ssem, rsem, target):
        copy = pltpu.make_async_remote_copy(
            src_ref=src, dst_ref=dst, send_sem=ssem, recv_sem=rsem, device_id=target, device_id_type=MESH
        )
        copy.start()
        sent.append(copy)
        return copy

    def settle(count):
        while len(sent) > count:
            sent.pop(0).wait_send()

    tile = (8, 128)
    sub, lane = sub_of(tile), lane_of(tile)
    slot = sub // 2

    line = lax.broadcasted_iota(jnp.int32, (512, 128), 0)
    col = lax.broadcasted_iota(jnp.int32, (512, 128), 1)
    face, pos = (col // 16) % 4, col % 16
    row_at, col_at = (line % 256) // PW, line % PW
    across = jnp.where(face < 2, row_at, col_at)
    along = jnp.where(face < 2, col_at, row_at)
    hit = (across == (face % 2) * (PW - 1)) & (along == pos) & (line // 256 == col // 64)
    pick[...] = jnp.where(hit, 1.0, 0.0).astype(BF16)

    def borders(values):
        low = values[0:7].reshape(FB, 256)
        high = jnp.concatenate([values[7:N], jnp.zeros((1, 8, 256), F32)], axis=0).reshape(FB, 256)
        wide = jnp.concatenate([low, high], axis=1)
        got = jnp.dot(three_parts(wide), pick[...], preferred_element_type=F32)
        return got[0:FB] + got[FB : 2 * FB] + got[2 * FB :]

    def z_send(ph, d, dist, hop):
        step = 1 - 2 * lax.rem(z, 2) if d == 0 else d
        at = lax.rem(z - step * (dist - hop) + NZ, NZ)
        return send(
            zgs[ph].at[at], zgs[ph].at[at], zss.at[ph, d + 1, dist - 1], zrs.at[ph, d + 1, dist - 1], z_dev(step * hop)
        )

    def z_step(ph, number, flying):
        waited, plan = (
            (0, ((4, 4), (3, 3), (2, 2), (1, 1))),
            (4, ((8, 4), (7, 3), (6, 2), (5, 1))),
        )[number]
        if waited:
            for d in (1, -1):
                flying.pop((d, waited)).wait_recv()
        for dist, hop in plan:
            for d in (0,) if dist == 8 else (1, -1):
                flying[(d, dist)] = z_send(ph, d, dist, hop)

    group = (lane_of((FB, 128)) // 16) % 4

    def choose(blocks):
        got = jnp.where(group == 1, blocks[0], jnp.where(group == 0, blocks[1], jnp.where(group == 3, blocks[2], blocks[3])))
        return got

    def y_phase(ph, flying):
        for copy in flying.values():
            copy.wait_recv()
        arriving = []
        for k in (2, 1, 3, 0):
            to = lax.rem(y + k, NY)
            block = choose([zgs[ph][tsm[to, 0, f] // NY] for f in range(4)])
            if k == 0:
                ybs[ph][y] = block
            else:
                ysend[ph, k - 1] = block
                arriving.append(
                    send(ysend.at[ph, k - 1], ybs[ph].at[y], yss.at[ph, k - 1], yrs.at[ph, k - 1], y_dev(k))
                )
        return arriving

    def ghosts(ph, arriving):
        for copy in arriving:
            copy.wait_recv()
        block = choose([ybs[ph][tsm[y, 0, f] % NY] for f in range(4)])
        got = jnp.dot(three_parts(block), spread[...], preferred_element_type=F32)
        got = got[0:FB] + got[FB : 2 * FB] + got[2 * FB :]
        return got

    def all_to_all(src, dst, rows, ssem, rsem):
        own = pl.multiple_of(place * rows, 8)
        arriving = []
        for k in (4, 3, 5, 2, 6, 1, 7):
            to = pl.multiple_of(lax.rem(place + k, NLINE) * rows, 8)
            arriving.append(
                send(src.at[pl.ds(to, rows)], dst.at[pl.ds(own, rows)], ssem.at[k - 1], rsem.at[k - 1], line_dev(k))
            )
        dst[pl.ds(own, rows)] = src[pl.ds(own, rows)]
        return arriving

    loads["prev"].wait()
    zg0[z] = borders(prev[...])
    tscr[y] = jnp.zeros(tile, jnp.int32)
    tscr[y, 0:2, 0:4] = tab_v[...]
    pl.semaphore_wait(barrier, len(friends))
    flying = {}
    z_step(0, 0, flying)
    tables = [send(tscr.at[y], tscr.at[y], tss.at[k - 1], trs.at[k - 1], y_dev(k)) for k in range(1, NY)]

    (uo, ue, pm, dd, v1, gl, gr, c1, sl, sr, x2, v2, g2, s2, c2, x3, v3, g3, s3, c3, rc, rd,
     w1, h1, x1r, w2, h2, w3, h3, w4) = [mats.at[n] for n in range(30)]

    def each_row(body):
        def step(i, carry):
            body(i)
            return carry

        lax.fori_loop(0, N, step, 0, unroll=True)

    first = ((sub < 2) & (place == 0))[None]
    even_sub = (sub % 2 == 0)[None]

    def build(i):
        e = edge[i].astype(F32)
        h0, h1 = e[:, :, :128], e[:, :, 128:]
        u = jnp.where(even_sub, h0, sroll(h1, 1))
        o = jnp.where(even_sub, sroll(h0, -1), h1)
        uo[i] = o
        ue[i] = jnp.where(first, 0.0, u)
        pm[i] = u + o
        dd[i] = o + jnp.where((sub < 6)[None], sroll(u, -2), 0.0)

    loads["edge"].wait()
    each_row(build)
    loads["damp"].wait()
    de, do = split_cells(damp[...])
    flag = flags[...].astype(F32)
    wall = jnp.where(sub == 0, flag[:, :128], flag[:, 128:])
    wall = jnp.where(first[0], wall, 0.0)
    for i in range(N):
        pm[i, i] = pm[i, i] + de[i] + wall * gain[i]
        dd[i, i] = dd[i, i] + do[i]
    inverse(pm, v1)
    mm(gl, v1, ue)
    mm(gr, v1, uo)
    mm_upper(sl, ue, gl)
    mm_upper(sr, uo, gr)
    mm(c1, ue, gr)

    def level(p, x, v, g, s, c, shift, between):
        inverse(p, v)
        mm(g, v, x)
        between()
        mm_upper(s, x, g)

        def turn(i):
            work[i] = sroll(g[i], -shift)

        each_row(turn)
        mm(c, x, work, True)

    def level_split(p, x, v, g, s, c, shift):
        inverse(p, v)
        xs, gs, ss, cs = [thin.at[n] for n in range(4)]
        quarter = lane // 32

        def split(k):
            for q in range(4):
                got = x[k, 4 * q]
                for n in range(1, min(4, N - 4 * q)):
                    got = jnp.where(quarter == n, x[k, 4 * q + n], got)
                xs[k, q] = got

        each_row(split)
        mm_split(gs, v, xs)
        mm_split(ss, x, gs, True, upper=True)
        if c is not None:
            mm_split(cs, x, gs, True, shift)

        def join(i):
            for q in range(4):
                wide = min(4, N - 4 * q)
                full = spread_groups(ss[i, q][None])
                far = spread_groups(cs[i, q][None]) if c is not None else None
                for n in range(wide):
                    g[i, 4 * q + n] = lroll(gs[i, q], -32 * n) if n else gs[i, q]
                    s[i, 4 * q + n] = full[n][0]
                    if c is not None:
                        c[i, 4 * q + n] = far[n][0]

        each_row(join)

    def build(i):
        d = dd[i] - sr[i] - jnp.where((sub < 6)[None], sroll(sl[i], -2), 0.0)
        dd[i] = d
        even = (slot % 2 == 0)[None]
        pm[i] = jnp.where(even, d, sroll(d, 2))
        x2[i] = jnp.where(even, c1[:, i], c1[i])

    each_row(build)
    level(pm, x2, v2, g2, s2, c2, 2, lambda: z_step(0, 1, flying))
    for copy in tables:
        copy.wait_recv()
    to_smem = pltpu.make_async_copy(tscr, tsm, lsem)
    to_smem.start()

    def build(i):
        d = dd[i] - s2[i] - jnp.where((slot == 1)[None], sroll(s2[i], -2), 0.0)
        dd[i] = d
        low = (slot == 0)[None]
        pm[i] = jnp.where(low, sroll(d, -2), sroll(d, 2))
        x3[i] = jnp.where(low, c2[:, i], c2[i])

    each_row(build)
    level(pm, x3, v3, g3, s3, c3, 4, lambda: None)

    def build(i):
        own = dd[i] - sroll(s3[i], 2)
        push = ue[:, i] - sl[:, i] - s2[:, i] - s3[:, i]
        cross = c3[i]
        rows = []
        for q in range(7):
            j = 2 * q
            parts = [cross[j], jnp.where(j >= i, sroll(own[j], 4), sroll(push[j], 2))]
            if j + 1 < N:
                parts += [sroll(cross[j + 1], 4), jnp.where(j + 1 >= i, own[j + 1], sroll(push[j + 1], -2))]
            else:
                parts += [jnp.zeros(tile, F32)] * 2
            v = parts[3]
            for t in range(3):
                v = jnp.where(slot == t, parts[t], v)
            rows.append(v[None])
        v = exchange_groups(jnp.concatenate(rows, axis=0))
        for q in range(7):
            fs[pl.ds(i * 7 + q, 8, stride=MROWS), :] = v[q]

    each_row(build)
    rows = []
    for q in range(4):
        v = jnp.zeros(tile, F32)
        for t in range(min(4, N - 4 * q)):
            i = 4 * q + t
            v = jnp.where(slot == t, sroll(ue[i, i] - sl[i, i] - s2[i, i] - s3[i, i], 2 * t), v)
        rows.append(v[None])
    v = exchange_groups(jnp.concatenate(rows, axis=0))
    for q in range(4):
        fs[pl.ds(91 + q, 8, stride=MROWS), :] = v[q]
    fs[pl.ds(95, 8, stride=MROWS), :] = jnp.zeros(tile, F32)
    blocks = all_to_all(fs, fr, MROWS, fss, frs)

    to_smem.wait()
    arriving = y_phase(0, flying)

    src = lax.broadcasted_iota(jnp.int32, (128, 1024), 0)
    dst = lax.broadcasted_iota(jnp.int32, (128, 1024), 1)
    face = ((src // 16) % 4) ^ 1
    turned = jnp.where(face == 0, tab_s[1, 0], jnp.where(face == 1, tab_s[1, 1], jnp.where(face == 2, tab_s[1, 2], tab_s[1, 3])))
    line = dst % 256
    across = jnp.where(face < 2, line // PW, line % PW)
    along = jnp.where(face < 2, line % PW, line // PW)
    along = along + turned * (PW - 1 - 2 * along)
    hit = (across == (face % 2) * (PW - 1)) & (along == src % 16)
    hit = hit & (dst // 512 == src // 64) & ((dst // 256) % 2 == face // 2)
    spread[...] = jnp.where(hit, 1.0, 0.0).astype(BF16)

    loads["lat"].wait()
    loads["res"].wait()
    for c in range(8):
        for h in range(2):
            lsc[h, pl.ds(4 * c, 4), :] = lat[c, :, pl.ds(128 * h, 128)]
    lats = [
        jnp.concatenate([lsc[h, pl.ds(d, 8, stride=4), :] for h in range(2)], axis=1) for d in range(4)
    ]
    line = lane_of((8, 256))
    edges = [line < PW, line >= 256 - PW, line % PW == 0, line % PW == PW - 1]
    for d in range(4):
        wts[d] = jnp.where(edges[d], 0.0, lats[d])
    for kind in range(2):
        wts[4 + kind] = jnp.where(
            edges[2 * kind], lats[2 * kind], jnp.where(edges[2 * kind + 1], lats[2 * kind + 1], 0.0)
        )

    def inside(v):
        for i in range(N):
            x = v[i]
            inner[i] = (
                wts[0] * lroll(x, PW) + wts[1] * lroll(x, -PW) + wts[2] * lroll(x, 1) + wts[3] * lroll(x, -1)
            )

    def right_side(got):
        weighted = []
        for i in range(N):
            at, base = (8 * i, 0) if i < 7 else (8 * (i - 7), 512)
            weighted.append(
                inner[i] + wts[4] * got[at : at + 8, base : base + 256] + wts[5] * got[at : at + 8, base + 256 : base + 512]
            )
        rows = []
        for a in range(N):
            acc = res[a]
            for b in range(N):
                acc = acc - coup[a, b] * weighted[b]
            rows.append(acc[None])
        return jnp.concatenate(rows, axis=0)

    def forward(ph, rhs):
        re, ro = split_cells(rhs)
        ul, ur = mvt(gl, re), mvt(gr, re)
        ro = ro + ur + jnp.where((sub < 6)[None], sroll(ul, -2), 0.0)
        rk2 = jnp.where((slot % 2 == 0)[None], ro, sroll(ro, 2))
        u2 = mvt(g2, rk2)
        ro = ro + u2 + jnp.where((slot == 1)[None], sroll(u2, -2), 0.0)
        rk3 = jnp.where((slot == 0)[None], sroll(ro, -2), sroll(ro, 2))
        u3 = mvt(g3, rk3)
        own = ro + sroll(u3, 2)
        tip = ul + u2 + u3
        rows = []
        for q in range(7):
            j = 2 * q
            v = jnp.where(slot == 0, tip[j], jnp.where(slot == 1, sroll(own[j], 4), 0.0))
            if j + 1 < N:
                v = jnp.where(slot == 2, sroll(tip[j + 1], 4), jnp.where(slot == 3, own[j + 1], v))
            rows.append(v[None])
        v = exchange_groups(jnp.concatenate(rows, axis=0))
        for q in range(7):
            vs[ph, pl.ds(q, 8, stride=VROWS), :] = v[q]
        vs[ph, pl.ds(7, 8, stride=VROWS), :] = jnp.zeros(tile, F32)
        arriving = all_to_all(vs.at[ph], vr.at[ph], VROWS, vss.at[ph], vrs.at[ph])
        return re, rk2, rk3, arriving

    def separators(ph, arriving):
        for copy in arriving:
            copy.wait_recv()
        got = [vr[ph, pl.ds(q, 8, stride=VROWS), :] for q in range(7)]
        tips = jnp.concatenate([(lroll(got[j // 2], 64) if j % 2 else got[j // 2])[None] for j in range(N)], axis=0)
        owns = jnp.concatenate([lroll(got[j // 2], 32 if j % 2 else 96)[None] for j in range(N)], axis=0)
        r = owns + jnp.where((sub < 7)[None], sroll(tips, -1), 0.0)
        even = (sub % 2 == 0)[None]
        fourth = (sub % 4 == 0)[None]
        rk1 = jnp.where(even, r, sroll(r, 1))
        u = mvt(h1, rk1)
        r = r + u + sroll(u, -1)
        rk2 = jnp.where(fourth, sroll(r, -1), sroll(r, 1))
        u = mvt(h2, rk2)
        r = r + sroll(u, 1) + sroll(u, -1)
        rk3 = sroll(r, 1)
        u = mvt(h3, rk3)
        x7 = mvt(w4, r + sroll(u, 3))
        x3 = sroll(mvt(w3, rk3) + mv(h3, sroll(x7, -3)), -1)
        known = jnp.where((sub == 3)[None], x3, x7)
        near = jnp.where((sub == 2)[None], sroll(x3, -1), jnp.where((sub == 4)[None], sroll(x3, 1), sroll(x7, -1)))
        near = jnp.where((sub == 0)[None], 0.0, near)
        u = mv(h2, near) + jnp.where(fourth, mvt(w2, rk2), 0.0)
        x = jnp.where((sub % 4 == 1)[None], sroll(u, 1) + sroll(u, -1), known)
        near = jnp.where((sub == 0)[None], 0.0, jnp.where(even, sroll(x, 1), x))
        u = mv(h1, near) + jnp.where(even, mvt(w1, rk1), 0.0)
        x = jnp.where(even, u + sroll(u, -1), x)
        below = jnp.where((sub == 0)[None], 0.0, sroll(x, 1))
        quarter = lane // 32
        for q in range(7):
            j = 2 * q
            v = jnp.where(quarter == 0, below[j], jnp.where(quarter == 1, lroll(x[j], 32), 0.0))
            if j + 1 < N:
                v = jnp.where(quarter == 2, lroll(below[j + 1], 64), jnp.where(quarter == 3, lroll(x[j + 1], 96), v))
            bs[ph, pl.ds(q, 8, stride=VROWS), :] = v
        bs[ph, pl.ds(7, 8, stride=VROWS), :] = jnp.zeros(tile, F32)
        return all_to_all(bs.at[ph], br.at[ph], VROWS, bss.at[ph], brs.at[ph])

    def backward(ph, kept, arriving):
        re, rk2, rk3, _ = kept
        y1, y2, y3 = mvt(v1, re), mvt(v2, rk2), mvt(v3, rk3)
        for copy in arriving:
            copy.wait_recv()
        got = jnp.concatenate([br[ph, pl.ds(q, 8, stride=VROWS), :][None] for q in range(7)], axis=0)
        got = exchange_groups(got)
        ends = []
        for j in range(N):
            v = got[j // 2]
            low, mid, top = (sroll(v, 4), sroll(v, -2), v) if j % 2 else (v, sroll(v, 2), sroll(v, 4))
            ends.append(jnp.where(slot == 0, low, jnp.where(slot == 2, mid, jnp.where(slot == 3, top, 0.0)))[None])
        ends = jnp.concatenate(ends, axis=0)
        u = mv(g3, ends) + jnp.where((slot == 0)[None], y3, 0.0)
        x3 = sroll(u, 2) + sroll(u, -2)
        near = jnp.where((slot == 1)[None], x3, jnp.where((slot == 2)[None], sroll(x3, 2), ends))
        u = mv(g2, near) + jnp.where((slot % 2 == 0)[None], y2, 0.0)
        both = u + sroll(u, -2)
        xo = jnp.where((slot % 2 == 0)[None], both, jnp.where((slot == 1)[None], x3, ends))
        xl = jnp.where((slot == 0)[None], ends, sroll(xo, 2))
        xe = y1 + mv(gl, xl) + mv(gr, xo)
        return join_cells(xe, xo)

    inside(prev)
    rhs = right_side(ghosts(0, arriving))
    kept = forward(0, rhs)

    rt = sr
    for copy in blocks:
        copy.wait_recv()

    def build(i):
        rows = [fr[pl.ds(i * 7 + q, 8, stride=MROWS), :][None] for q in range(7)]
        got = spread_groups(jnp.concatenate(rows, axis=0))
        for j in range(N):
            rc[i, j] = got[j % 2 * 2][j // 2]
            rt[i, j] = got[j % 2 * 2 + 1][j // 2]

    each_row(build)

    def build(i):
        rd[i] = rt[i] + jnp.where((sub < 7)[None], sroll(rt[:, i], -1), 0.0)

    each_row(build)
    rows = [fr[pl.ds(91 + q, 8, stride=MROWS), :][None] for q in range(4)]
    got = spread_groups(jnp.concatenate(rows, axis=0))
    for i in range(N):
        rd[i, i] = rt[i, i] + jnp.where(sub < 7, sroll(got[i % 4][i // 4], -1), 0.0)

    def build(i):
        even = (sub % 2 == 0)[None]
        x1r[i] = jnp.where(even, rc[:, i], rc[i])
        pm[i] = jnp.where(even, rd[i], sroll(rd[i], 1))

    each_row(build)
    level_split(pm, x1r, w1, h1, s3, c3, 1)

    def build(i):
        d = rd[i] - s3[i] - sroll(s3[i], -1)
        rd[i] = d
        fourth = (sub % 4 == 0)[None]
        pm[i] = jnp.where(fourth, sroll(d, -1), sroll(d, 1))
        x2[i] = jnp.where(fourth, c3[:, i], c3[i])

    each_row(build)
    level_split(pm, x2, w2, h2, s3, c2, 2)

    def build(i):
        d = rd[i] - sroll(s3[i], 1) - sroll(s3[i], -1)
        rd[i] = d
        pm[i] = sroll(d, 1)

    each_row(build)
    level_split(pm, c2, w3, h3, s3, None, 0)

    def build(i):
        pm[i] = rd[i] - sroll(s3[i], 3)

    each_row(build)
    inverse(pm, w4)

    back = separators(0, kept[3])
    first_sweep = backward(0, kept, back)
    zg1[z] = borders(first_sweep)
    field[...] = first_sweep
    flying = {}
    z_step(1, 0, flying)
    inside(field)
    settle(8)
    z_step(1, 1, flying)
    arriving = y_phase(1, flying)
    settle(3)
    rhs = right_side(ghosts(1, arriving))
    kept = forward(1, rhs)
    settle(7)
    back = separators(1, kept[3])
    settle(7)
    out[...] = backward(1, kept, back)

    settle(0)


def body(residual, previous, edge_blocks, damping, lateral, coupling, wall_flags, wall_gain, face_table):
    def by_unknown(v):
        return jnp.transpose(v, (1, 0, 2))

    table = jnp.transpose(face_table[0])
    vmem = pl.BlockSpec(memory_space=pltpu.VMEM)
    smem = pl.BlockSpec(memory_space=pltpu.SMEM)
    far = pl.BlockSpec(memory_space=pl.ANY)
    dma = pltpu.SemaphoreType.DMA
    got = pl.pallas_call(
        kernel,
        out_shape=jax.ShapeDtypeStruct((N, 8, 256), F32),
        in_specs=[far, far, far, far, far, smem, vmem, smem, vmem, smem],
        out_specs=vmem,
        scratch_shapes=[
            pltpu.VMEM((N, 8, 256), F32),
            pltpu.VMEM((N, 8, 256), F32),
            pltpu.VMEM((N, N, 8, 256), BF16),
            pltpu.VMEM((N, 8, 256), F32),
            pltpu.VMEM((8, 4, 256), F32),
            dma((5,)),
            pltpu.VMEM((30, N, N, 8, 128), F32),
            pltpu.VMEM((N, N, 8, 128), F32),
            pltpu.VMEM((4, N, 4, 8, 128), F32),
            pltpu.VMEM((NZ, FB, 128), F32),
            pltpu.VMEM((NZ, FB, 128), F32),
            pltpu.VMEM((NY, FB, 128), F32),
            pltpu.VMEM((NY, FB, 128), F32),
            pltpu.VMEM((2, NY - 1, FB, 128), F32),
            pltpu.VMEM((NY, 8, 128), jnp.int32),
            pltpu.SMEM((NY, 8, 128), jnp.int32),
            pltpu.VMEM((512, 128), BF16),
            pltpu.VMEM((128, 1024), BF16),
            pltpu.VMEM((2, 32, 128), F32),
            pltpu.VMEM((6, 8, 256), F32),
            pltpu.VMEM((N, 8, 256), F32),
            pltpu.VMEM((N, 8, 256), F32),
            pltpu.VMEM((NLINE * MROWS, 128), F32),
            pltpu.VMEM((NLINE * MROWS, 128), F32),
            pltpu.VMEM((2, NLINE * VROWS, 128), F32),
            pltpu.VMEM((2, NLINE * VROWS, 128), F32),
            pltpu.VMEM((2, NLINE * VROWS, 128), F32),
            pltpu.VMEM((2, NLINE * VROWS, 128), F32),
            dma((2, 3, 8)),
            dma((2, 3, 8)),
            dma((2, NY - 1)),
            dma((2, NY - 1)),
            dma((NY - 1,)),
            dma((NY - 1,)),
            dma((NLINE - 1,)),
            dma((NLINE - 1,)),
            dma((2, NLINE - 1)),
            dma((2, NLINE - 1)),
            dma((2, NLINE - 1)),
            dma((2, NLINE - 1)),
            dma,
        ],
        compiler_params=pltpu.CompilerParams(
            collective_id=0, has_side_effects=True, vmem_limit_bytes=58 * 1024 * 1024
        ),
        name="line_sweeps",
    )(
        by_unknown(residual),
        by_unknown(previous),
        jnp.transpose(edge_blocks, (1, 2, 0, 3)),
        by_unknown(damping),
        lateral,
        coupling,
        wall_flags.reshape(1, 256),
        wall_gain,
        table,
        table,
    )
    return jnp.transpose(got, (1, 0, 2))


def solution(mesh):
    placed = (
        P("line", None, "surf"),
        P("line", None, "surf"),
        P("line", None, None, "surf"),
        P("line", None, "surf"),
        P("line", None, "surf"),
        P(),
        P("surf"),
        P(),
        P("surf", None, None),
    )
    return jax.shard_map(
        body, mesh=mesh, in_specs=placed, out_specs=P("line", None, "surf"), check_vma=False
    )
```
